32 devices in a mesh: blk: 16 (over z, x, core), group: 2 (over y).
Axes of the slice: x: 2, y: 2, z: 4, core: 2. Of those that a mesh axis runs over, the one named last changes fastest.
Arguments:
- audio_features: bfloat16 [4096, 768], P(('blk', 'group')), may hold values from -6 to 6
- audio_weight: bfloat16 [768, 512], replicated, may hold values from -0.21875 to 0.21875
- text_features: bfloat16 [4096, 768], P(('blk', 'group')), may hold values from -6 to 6
- text_weight: bfloat16 [768, 512], replicated, may hold values from -0.21875 to 0.21875
- logit_scale: float32 [1], replicated, may hold values from 10 to 30
- logit_bias: float32 [1], replicated, may hold values from -6 to -2
Outputs:
- audio_weight_grad: float32 [768, 512], replicated
- text_weight_grad: float32 [768, 512], replicated
The draws below stay inside these ranges and needn't reach their ends.
All inputs are finite; a program needn't handle non-finite values.
Results may differ from the reference program's by a relative error of at most 0.0029.
Values may be sent and summed in bfloat16 or wider, within the bound.
A program may use at most 64 MiB of HBM per device.

```python
import math
import jax
import jax.numpy as jnp
from jax import lax

D = 512
FA = 768
FT = 768
ROWS = 128
PAIRS = 4096
N_GROUP = 2


def block_levels(key, extent, shards, least, high):
    level, own = 1.0, jax.random.fold_in(key, 6)
    for axis_at, shards_of in shards:
        steps = jnp.exp(jax.random.uniform(jax.random.fold_in(own, axis_at), (shards_of,), jnp.float32, least / len(shards), high / len(shards)))
        level = level * jnp.repeat(steps, extent[axis_at] // shards_of).reshape([-1 if axis == axis_at else 1 for axis in range(len(extent))])
    return level


def scatter_about(rng, extent, scale, limit, shards=(), kind=jnp.bfloat16):
    values = jax.random.normal(rng, extent, jnp.float32) * scale
    if len(shards) > 0:
        values = block_levels(rng, extent, shards, -0.22, 0.18) * values
    return jnp.clip(values, min=-limit, max=limit).astype(kind)


def setup_inputs(seed: int = 0) -> dict:
    splits = jax.random.split(jax.random.key(seed), 7)
    audio_features = scatter_about(splits[0], (PAIRS, FA), 1.0, 6.0, ((0, 32),))
    audio_weight = scatter_about(splits[1], (FA, D), FA ** -0.5, 0.21875)
    text_features = scatter_about(splits[2], (PAIRS, FT), 1.0, 6.0, ((0, 32),))
    text_weight = scatter_about(splits[3], (FT, D), FT ** -0.5, 0.21875)
    logit_scale = jnp.clip(jnp.exp(jax.random.uniform(splits[4], (1,), jnp.float32, math.log(10.0), math.log(30.0))), 10.0, 30.0)
    logit_bias = jnp.clip(jax.random.uniform(splits[5], (1,), jnp.float32, -6.0, -2.0), -6.0, -2.0)
    return dict(audio_features=audio_features, audio_weight=audio_weight, text_features=text_features, text_weight=text_weight, logit_scale=logit_scale, logit_bias=logit_bias)


EPSILON = 1e-06

def embed(features, weight):
    hidden = jnp.dot(features, weight, preferred_element_type=jnp.float32)
    norm_value = jnp.sqrt(lax.optimization_barrier(jnp.sum(hidden * hidden, axis=1, keepdims=True)) + EPSILON)
    return (hidden / norm_value, norm_value)

def unit_backward(grad, unit, norm_value):
    return (grad - unit * lax.optimization_barrier(jnp.sum(unit * grad, axis=1, keepdims=True))) / norm_value

def weight_grad(features, hidden_grad):
    high_part = hidden_grad.astype(jnp.bfloat16)
    low_part = (hidden_grad - high_part.astype(jnp.float32)).astype(jnp.bfloat16)
    dims = (((0,), (0,)), ((), ()))
    first = lax.dot_general(features, high_part, dims, preferred_element_type=jnp.float32)
    second = lax.dot_general(features, low_part, dims, preferred_element_type=jnp.float32)
    return first + second

def reference(audio_features, audio_weight, text_features, text_weight, logit_scale, logit_bias):
    clip_unit, clip_norm = embed(audio_features, audio_weight)
    text_unit, text_norm = embed(text_features, text_weight)
    clips = clip_unit.astype(jnp.bfloat16)
    texts = text_unit.astype(jnp.bfloat16)
    block_rows = ROWS * N_GROUP
    block_count = PAIRS // block_rows
    temper = logit_scale[0]
    offset = logit_bias[0]
    columns = jnp.arange(PAIRS, dtype=jnp.int32)

    def step(text_total, index):
        start = (index * block_rows).astype(jnp.int32)
        clip_block = lax.dynamic_slice_in_dim(clips, start, block_rows, 0)
        logits = temper * jnp.dot(clip_block, texts.T, preferred_element_type=jnp.float32) + offset
        row_index = start + jnp.arange(block_rows, dtype=jnp.int32)
        sign = jnp.where(row_index[:, None] == columns[None, :], 1.0, -1.0).astype(logits.dtype)
        gate = (-sign * jax.nn.sigmoid(-sign * logits)).astype(jnp.bfloat16)
        clip_part = temper * jnp.dot(gate, texts, preferred_element_type=jnp.float32)
        text_total = text_total + temper * jnp.dot(gate.T, clip_block, preferred_element_type=jnp.float32)
        return (text_total, clip_part)
    text_grad, clip_parts = lax.scan(step, jnp.zeros((PAIRS, D), jnp.float32), jnp.arange(block_count, dtype=jnp.int32))
    clip_grad = clip_parts.reshape(PAIRS, D)
    audio_hidden_grad = unit_backward(clip_grad, clip_unit, clip_norm)
    text_hidden_grad = unit_backward(text_grad, text_unit, text_norm)
    return (weight_grad(audio_features, audio_hidden_grad), weight_grad(text_features, text_hidden_grad))
```

```python
import functools

import jax
import jax.numpy as jnp
from jax import lax
from jax.experimental import pallas as pl
from jax.experimental.pallas import tpu as pltpu
from jax.sharding import PartitionSpec as P

EPSILON = 1e-06
BF16 = jnp.bfloat16
F32 = jnp.float32
INNER = 4
TN = (((0,), (0,)), ((), ()))
NT = (((1,), (1,)), ((), ()))


def kernel(
    blocks, groups,
    audio_ref, audio_w_ref, text_ref, text_w_ref, scale_ref, bias_ref,
    out_ref,
    clips, texts, staged, feats, gates, clip_send, clip_recv, text_send, text_recv,
    clip_own, text_own, units, norms, hid_send, hid_recv, partial, part_recv,
    s_clip, r_clip, s_text, r_text, s_feat, r_feat, s_cg, r_cg, s_tg, r_tg,
    s_hid, r_hid, s_part, r_part, s_agz, r_agz, s_agp, r_agp, s_agc, r_agc,
):
    depth = blocks // INNER
    plane = INNER * groups
    rows = audio_ref.shape[0]
    width = audio_w_ref.shape[1]
    lanes = width // 4
    span = audio_w_ref.shape[0] // depth
    blk = lax.axis_index("blk")
    group = lax.axis_index("group")
    zed = lax.div(blk, INNER)
    inner = lax.rem(blk, INNER)
    me = inner * groups + group

    def at_plane(a):
        return (zed * INNER + lax.div(a, groups), lax.rem(a, groups))

    def at_depth(z):
        return (z * INNER + inner, group)

    def role(a):
        i, g = lax.div(a, groups), lax.rem(a, groups)
        return lax.rem(i, 2) * 4 + lax.div(i, 2) * 2 + lax.rem(g, 2)

    def copy(src, dst, send, recv, device):
        return pltpu.make_async_remote_copy(
            src_ref=src, dst_ref=dst, send_sem=send, recv_sem=recv,
            device_id=device, device_id_type=pl.DeviceIdType.MESH,
        )

    def peers(count, own, fn):
        def body(k, carry):
            fn(lax.rem(own + k, count))
            return carry
        lax.fori_loop(1, count, body, 0)

    mine = role(me)
    kind = lax.div(mine, 4)
    part = lax.rem(mine, 4)

    barrier = pltpu.get_barrier_semaphore()
    peers(plane, me, lambda a: pl.semaphore_signal(
        barrier, inc=1, device_id=at_plane(a), device_id_type=pl.DeviceIdType.MESH))
    peers(depth, zed, lambda z: pl.semaphore_signal(
        barrier, inc=1, device_id=at_depth(z), device_id_type=pl.DeviceIdType.MESH))

    def embed(at, features, weight):
        hidden = jnp.dot(features[...], weight[...], preferred_element_type=F32)
        norm = jnp.sqrt(jnp.sum(hidden * hidden, axis=1, keepdims=True) + EPSILON)
        unit = hidden / norm
        units[at] = unit
        norms[at] = jnp.broadcast_to(norm, (rows, 128))
        return unit.astype(BF16)

    texts[zed] = embed(1, text_ref, text_w_ref)
    pl.semaphore_wait(barrier, plane - 1 + depth - 1)

    def send_text(z):
        copy(texts.at[zed], texts.at[zed], s_text.at[z], r_text.at[zed], at_depth(z)).start()
    peers(depth, zed, send_text)

    clips[me] = embed(0, audio_ref, audio_w_ref)

    def send_clip(a):
        copy(clips.at[me], clips.at[me], s_clip.at[a], r_clip.at[me], at_plane(a)).start()
    peers(plane, me, send_clip)

    staged[0] = audio_ref[...]
    staged[1] = text_ref[...]
    feats[me] = staged[kind]

    def got(buf, at, recv, send):
        copy(buf.at[at], buf.at[at], send.at[at], recv.at[at], (blk, group)).wait_recv()

    peers(depth, zed, lambda z: got(texts, z, r_text, s_text))

    scale = scale_ref[0]
    bias = bias_ref[0]
    all_texts = lambda: texts[...].reshape(depth * rows, width)

    def gate_block(a, own):
        logits = scale * lax.dot_general(clips[a], all_texts(), NT, preferred_element_type=F32) + bias
        if own:
            row = lax.broadcasted_iota(jnp.int32, logits.shape, 0)
            column = lax.broadcasted_iota(jnp.int32, logits.shape, 1)
            sign = jnp.where(column - row == zed * rows, 1.0, -1.0)
            gate = (-sign / (1.0 + jnp.exp(sign * logits))).astype(BF16)
        else:
            gate = (1.0 / (1.0 + jnp.exp(-logits))).astype(BF16)
        gates[a] = gate
        return jnp.dot(gate, all_texts(), preferred_element_type=F32)

    clip_own[...] = gate_block(me, True)

    def clip_step(a):
        got(clips, a, r_clip, s_clip)
        clip_send[a] = gate_block(a, False).astype(BF16)
        copy(clip_send.at[a], clip_recv.at[me], s_cg.at[a], r_cg.at[me], at_plane(a)).start()
    peers(plane, me, clip_step)

    def text_term(z):
        start = pl.multiple_of(z * rows, rows)
        block = gates[:, :, pl.ds(start, rows)].reshape(plane * rows, rows)
        return lax.dot_general(
            block, clips[...].reshape(plane * rows, width), TN, preferred_element_type=F32)

    def text_step(z):
        text_send[z] = text_term(z).astype(BF16)
        copy(text_send.at[z], text_recv.at[zed], s_tg.at[z], r_tg.at[zed], at_depth(z)).start()
    peers(depth, zed, text_step)

    def send_feat(a):
        copy(staged.at[lax.div(role(a), 4)], feats.at[me], s_feat.at[a], r_feat.at[me], at_plane(a)).start()
    peers(plane, me, send_feat)

    text_own[...] = text_term(zed)

    def backward(at, own, grad):
        unit = units[at]
        grad = scale * grad
        inner_sum = jnp.sum(unit * grad, axis=1, keepdims=True)
        result = (grad - unit * inner_sum) / norms[at][:, :1]
        for s in range(4):
            hid_send[4 * at + s] = result[:, s * lanes:(s + 1) * lanes]

    def add_clip(a):
        got(clip_recv, a, r_cg, s_cg)
        clip_own[...] += clip_recv[a].astype(F32)
    peers(plane, me, add_clip)
    backward(0, clip_own, clip_own[...])

    def send_hid(want, a):
        @pl.when(lax.div(role(a), 4) == want)
        def _():
            copy(hid_send.at[role(a)], hid_recv.at[me], s_hid.at[a], r_hid.at[me], at_plane(a)).start()
    peers(plane, me, functools.partial(send_hid, 0))

    def add_text(z):
        got(text_recv, z, r_tg, s_tg)
        text_own[...] += text_recv[z].astype(F32)
    peers(depth, zed, add_text)
    backward(1, text_own, text_own[...])
    peers(plane, me, functools.partial(send_hid, 1))
    hid_recv[me] = hid_send[mine]

    peers(plane, me, lambda a: got(feats, a, r_feat, s_feat))
    peers(plane, me, lambda a: got(hid_recv, a, r_hid, s_hid))
    hidden = hid_recv[...].reshape(plane * rows, lanes)
    high = hidden.astype(BF16)
    low = (hidden - high.astype(F32)).astype(BF16)
    both = lax.dot_general(
        feats[...].reshape(plane * rows, feats.shape[2]),
        jnp.concatenate([high, low], axis=1), TN, preferred_element_type=F32)
    partial[...] = (both[:, :lanes] + both[:, lanes:]).reshape(partial.shape)

    def send_part(z):
        copy(partial.at[z], part_recv.at[zed], s_part.at[z], r_part.at[zed], at_depth(z)).start()
    peers(depth, zed, send_part)
    part_recv[zed] = partial[zed]
    peers(depth, zed, lambda z: got(part_recv, z, r_part, s_part))
    total = part_recv[0]
    for z in range(1, depth):
        total = total + part_recv[z]

    def piece(k, p, z):
        return out_ref.at[k, p, pl.ds(pl.multiple_of(z * span, span), span)]

    out_ref[kind, part, pl.ds(pl.multiple_of(zed * span, span), span)] = total.astype(BF16)

    near = lax.div(group, 2) * 2
    sibling = (zed * INNER + inner + 1 - 2 * kind, group)

    def same_core(p):
        return (zed * INNER + lax.div(p, 2) * 2 + kind, near + lax.rem(p, 2))

    def send_z(z):
        copy(piece(kind, part, zed), piece(kind, part, zed), s_agz.at[z], r_agz.at[zed], at_depth(z)).start()
    peers(depth, zed, send_z)

    def to_sibling(p, z):
        here = piece(kind, p, z)
        copy(here, here, s_agc.at[p, z], r_agc.at[p, z], sibling).start()

    def spread(z):
        here = piece(kind, part, z)

        def send(p):
            copy(here, here, s_agp.at[p, z], r_agp.at[part, z], same_core(p)).start()
        peers(4, part, send)
        to_sibling(part, z)

    spread(zed)

    def take_z(z):
        here = piece(kind, part, z)
        copy(here, here, s_agz.at[z], r_agz.at[z], (blk, group)).wait_recv()
        spread(z)
    peers(depth, zed, take_z)

    def relay(k, carry):
        z = lax.rem(zed + k, depth)

        def take(p):
            here = piece(kind, p, z)
            copy(here, here, s_agp.at[p, z], r_agp.at[p, z], (blk, group)).wait_recv()
            to_sibling(p, z)
        peers(4, part, take)
        return carry
    lax.fori_loop(0, depth, relay, 0)

    def finish(k, carry):
        z = lax.rem(zed + k, depth)
        for p in range(4):
            there = piece(1 - kind, p, z)
            copy(there, there, s_agc.at[p, z], r_agc.at[p, z], sibling).wait_recv()
        return carry
    lax.fori_loop(0, depth, finish, 0)

    def sent(src, send, recv, at):
        copy(src, src, send.at[at], recv.at[at], (blk, group)).wait_send()

    def drain_plane(a):
        sent(clips.at[me], s_clip, r_clip, a)
        sent(staged.at[0], s_feat, r_feat, a)
        sent(clip_send.at[a], s_cg, r_cg, a)
        sent(hid_send.at[0], s_hid, r_hid, a)
    peers(plane, me, drain_plane)

    def drain_depth(z):
        sent(texts.at[zed], s_text, r_text, z)
        sent(text_send.at[z], s_tg, r_tg, z)
        sent(partial.at[z], s_part, r_part, z)
        sent(piece(kind, part, zed), s_agz, r_agz, z)
    peers(depth, zed, drain_depth)

    def drain_out(z, carry):
        def one(p):
            here = piece(kind, part, z)
            copy(here, here, s_agp.at[p, z], r_agp.at[p, z], (blk, group)).wait_send()
        peers(4, part, one)
        for p in range(4):
            here = piece(kind, p, z)
            copy(here, here, s_agc.at[p, z], r_agc.at[p, z], sibling).wait_send()
        return carry
    lax.fori_loop(0, depth, drain_out, 0)


def per_device(blocks, groups, audio, audio_w, text, text_w, scale, bias):
    rows, wide = audio.shape
    width = audio_w.shape[1]
    depth, plane = blocks // INNER, INNER * groups
    lanes, span = width // 4, wide // depth
    vmem = pl.BlockSpec(memory_space=pltpu.VMEM)
    smem = pl.BlockSpec(memory_space=pltpu.SMEM)
    dma = pltpu.SemaphoreType.DMA
    sems = []
    for count in (plane, depth, plane, plane, depth, plane, depth, depth):
        sems += [dma((count,)), dma((count,))]
    sems += [dma((4, depth))] * 4
    out = pl.pallas_call(
        functools.partial(kernel, blocks, groups),
        out_shape=jax.ShapeDtypeStruct((2, 4, wide, lanes), BF16),
        in_specs=[vmem, vmem, vmem, vmem, smem, smem],
        out_specs=vmem,
        scratch_shapes=[
            pltpu.VMEM((plane, rows, width), BF16),
            pltpu.VMEM((depth, rows, width), BF16),
            pltpu.VMEM((2, rows, wide), BF16),
            pltpu.VMEM((plane, rows, wide), BF16),
            pltpu.VMEM((plane, rows, depth * rows), BF16),
            pltpu.VMEM((plane, rows, width), BF16),
            pltpu.VMEM((plane, rows, width), BF16),
            pltpu.VMEM((depth, rows, width), BF16),
            pltpu.VMEM((depth, rows, width), BF16),
            pltpu.VMEM((rows, width), F32),
            pltpu.VMEM((rows, width), F32),
            pltpu.VMEM((2, rows, width), F32),
            pltpu.VMEM((2, rows, 128), F32),
            pltpu.VMEM((8, rows, lanes), F32),
            pltpu.VMEM((plane, rows, lanes), F32),
            pltpu.VMEM((depth, span, lanes), F32),
            pltpu.VMEM((depth, span, lanes), F32),
        ] + sems,
        compiler_params=pltpu.CompilerParams(
            collective_id=0, has_side_effects=True, vmem_limit_bytes=56 * 1024 * 1024),
    )(audio, audio_w, text, text_w, scale, bias)
    whole = out.astype(F32).transpose(0, 2, 1, 3).reshape(2, wide, width)
    return whole[0], whole[1]


def solution(mesh):
    placed = (P(("blk", "group"), None), P(), P(("blk", "group"), None), P(), P(), P())
    step = functools.partial(per_device, mesh.shape["blk"], mesh.shape["group"])
    return jax.shard_map(step, mesh=mesh, in_specs=placed, out_specs=(P(), P()), check_vma=False)
```

```python
import functools

import jax
import jax.numpy as jnp
from jax import lax
from jax.experimental import pallas as pl
from jax.experimental.pallas import tpu as pltpu
from jax.sharding import PartitionSpec as P

EPSILON = 1e-06
BF16 = jnp.bfloat16
F32 = jnp.float32
INNER = 4
TN = (((0,), (0,)), ((), ()))
NT = (((1,), (1,)), ((), ()))


def kernel(
    blocks, groups,
    audio_ref, audio_w_ref, text_ref, text_w_ref, scale_ref, bias_ref,
    audio_out, text_out,
    clips, texts, staged, weights, feats, gates, clip_send, clip_recv, text_send, text_recv,
    clip_own, text_own, units, norms, hid_send, hid_recv, part_own, part_send, part_recv, gathered,
    s_in, s_clip, s_clipf, r_clip, s_text, r_text, s_feat, s_featf, r_feat, s_cg, r_cg, s_tg, r_tg,
    s_hid, r_hid, s_part, r_part, s_agz, r_agz, s_agp, r_agp, s_agc, r_agc,
):
    depth = blocks // INNER
    plane = INNER * groups
    rows = audio_ref.shape[0]
    width = audio_w_ref.shape[1]
    lanes = width // 4
    span = audio_w_ref.shape[0] // depth
    blk = lax.axis_index("blk")
    group = lax.axis_index("group")
    zed = lax.div(blk, INNER)
    inner = lax.rem(blk, INNER)
    me = inner * groups + group

    def at_plane(a):
        return (zed * INNER + lax.div(a, groups), lax.rem(a, groups))

    def at_depth(z):
        return (z * INNER + inner, group)

    half = plane // 2
    core = lax.rem(inner, 2)
    pos = lax.div(inner, 2) * groups + group
    sibling = (zed * INNER + inner + 1 - 2 * core, group)

    def block_at(q, c):
        return (lax.div(q, groups) * 2 + c) * groups + lax.rem(q, groups)

    def kind_of(a):
        return lax.rem(lax.rem(a, groups), 2)

    def role(a):
        return kind_of(a) * 4 + lax.div(a, groups)

    sources = (audio_ref, text_ref, audio_w_ref, text_w_ref)
    targets = (staged.at[0], staged.at[1], weights.at[0], weights.at[1])
    loads = [pltpu.make_async_copy(sources[k], targets[k], s_in.at[k]) for k in range(4)]
    for k in (1, 3, 0, 2):
        loads[k].start()

    def copy(src, dst, send, recv, device):
        return pltpu.make_async_remote_copy(
            src_ref=src, dst_ref=dst, send_sem=send, recv_sem=recv,
            device_id=device, device_id_type=pl.DeviceIdType.MESH,
        )

    def peers(count, own, fn):
        def body(k, carry):
            fn(lax.rem(own + k, count))
            return carry
        lax.fori_loop(1, count, body, 0)

    mine = role(me)
    kind = kind_of(me)

    barrier = pltpu.get_barrier_semaphore()
    peers(plane, me, lambda a: pl.semaphore_signal(
        barrier, inc=1, device_id=at_plane(a), device_id_type=pl.DeviceIdType.MESH))
    peers(depth, zed, lambda z: pl.semaphore_signal(
        barrier, inc=1, device_id=at_depth(z), device_id_type=pl.DeviceIdType.MESH))

    def embed(at):
        hidden = jnp.dot(staged[at], weights[at], preferred_element_type=F32)
        norm = jnp.sqrt(jnp.sum(hidden * hidden, axis=1, keepdims=True) + EPSILON)
        unit = hidden / norm
        units[at] = unit
        norms[at] = jnp.broadcast_to(norm, (rows, 128))
        return unit.astype(BF16)

    loads[1].wait()
    loads[3].wait()
    texts[zed] = embed(1)
    pl.semaphore_wait(barrier, plane - 1 + depth - 1)

    def send_text(z):
        copy(texts.at[zed], texts.at[zed], s_text.at[z], r_text.at[zed], at_depth(z)).start()
    peers(depth, zed, send_text)

    loads[0].wait()
    loads[2].wait()
    clips[me] = embed(0)

    def send_clip(q):
        copy(clips.at[me], clips.at[me], s_clip.at[q], r_clip.at[me], at_plane(block_at(q, core))).start()
    peers(half, pos, send_clip)
    copy(clips.at[me], clips.at[me], s_clipf.at[pos], r_clip.at[me], sibling).start()

    feats[me] = staged[kind]

    def send_feat(q):
        a = block_at(q, core)
        copy(staged.at[kind_of(a)], feats.at[me], s_feat.at[q], r_feat.at[me], at_plane(a)).start()
    peers(half, pos, send_feat)
    copy(staged.at[kind], feats.at[me], s_featf.at[pos], r_feat.at[me], sibling).start()

    def got(buf, at, recv, send):
        copy(buf.at[at], buf.at[at], send.at[0], recv.at[at], (blk, group)).wait_recv()

    def pass_clip(q):
        a = block_at(q, core)
        got(clips, a, r_clip, s_clip)
        copy(clips.at[a], clips.at[a], s_clipf.at[q], r_clip.at[a], sibling).start()
    peers(half, pos, pass_clip)

    peers(depth, zed, lambda z: got(texts, z, r_text, s_text))

    scale = scale_ref[0]
    bias = bias_ref[0]
    all_texts = lambda: texts[...].reshape(depth * rows, width)

    def gate_block(a, own):
        logits = scale * lax.dot_general(clips[a], all_texts(), NT, preferred_element_type=F32) + bias
        if own:
            row = lax.broadcasted_iota(jnp.int32, logits.shape, 0)
            column = lax.broadcasted_iota(jnp.int32, logits.shape, 1)
            sign = jnp.where(column - row == zed * rows, 1.0, -1.0)
            gate = (-sign / (1.0 + jnp.exp(sign * logits))).astype(BF16)
        else:
            gate = (1.0 / (1.0 + jnp.exp(-logits))).astype(BF16)
        gates[a] = gate
        return jnp.dot(gate, all_texts(), preferred_element_type=F32)

    clip_own[...] = gate_block(me, True)

    def clip_step(a):
        clip_send[a] = gate_block(a, False).astype(BF16)
        copy(clip_send.at[a], clip_recv.at[me], s_cg.at[a], r_cg.at[me], at_plane(a)).start()
    peers(half, pos, lambda q: clip_step(block_at(q, core)))

    def clip_other(q, carry):
        a = block_at(q, 1 - core)
        got(clips, a, r_clip, s_clip)
        clip_step(a)
        return carry
    lax.fori_loop(0, half, clip_other, 0)

    def text_term(z):
        start = pl.multiple_of(z * rows, rows)
        block = gates[:, :, pl.ds(start, rows)].reshape(plane * rows, rows)
        return lax.dot_general(
            block, clips[...].reshape(plane * rows, width), TN, preferred_element_type=F32)

    def text_step(z):
        text_send[z] = text_term(z).astype(BF16)
        copy(text_send.at[z], text_recv.at[zed], s_tg.at[z], r_tg.at[zed], at_depth(z)).start()
    peers(depth, zed, text_step)

    def pass_feat(q):
        a = block_at(q, core)
        got(feats, a, r_feat, s_feat)
        copy(feats.at[a], feats.at[a], s_featf.at[q], r_feat.at[a], sibling).start()
    peers(half, pos, pass_feat)

    text_own[...] = text_term(zed)

    def backward(at, own, grad):
        unit = units[at]
        grad = scale * grad
        inner_sum = jnp.sum(unit * grad, axis=1, keepdims=True)
        result = (grad - unit * inner_sum) / norms[at][:, :1]
        for s in range(4):
            hid_send[4 * at + s] = result[:, s * lanes:(s + 1) * lanes]

    def add_clip(a):
        got(clip_recv, a, r_cg, s_cg)
        clip_own[...] += clip_recv[a].astype(F32)
    peers(plane, me, add_clip)
    backward(0, clip_own, clip_own[...])

    def send_hid(want, a):
        @pl.when(kind_of(a) == want)
        def _():
            copy(hid_send.at[role(a)], hid_recv.at[me], s_hid.at[a], r_hid.at[me], at_plane(a)).start()
    peers(plane, me, functools.partial(send_hid, 0))

    def add_text(z):
        got(text_recv, z, r_tg, s_tg)
        text_own[...] += text_recv[z].astype(F32)
    peers(depth, zed, add_text)
    backward(1, text_own, text_own[...])
    peers(plane, me, functools.partial(send_hid, 1))
    hid_recv[me] = hid_send[mine]

    def take_feat(q, carry):
        got(feats, block_at(q, 1 - core), r_feat, s_feat)
        return carry
    lax.fori_loop(0, half, take_feat, 0)
    peers(plane, me, lambda a: got(hid_recv, a, r_hid, s_hid))
    hidden = hid_recv[...].reshape(plane * rows, lanes)
    high = hidden.astype(BF16)
    low = (hidden - high.astype(F32)).astype(BF16)
    both = lax.dot_general(
        feats[...].reshape(plane * rows, feats.shape[2]),
        jnp.concatenate([high, low], axis=1), TN, preferred_element_type=F32)
    terms = (both[:, :lanes] + both[:, lanes:]).reshape(part_own.shape)
    part_own[...] = terms
    part_send[...] = terms.astype(BF16)

    def send_part(z):
        copy(part_send.at[z], part_recv.at[zed], s_part.at[z], r_part.at[zed], at_depth(z)).start()
    peers(depth, zed, send_part)
    part_recv[zed] = jnp.zeros(part_recv.shape[1:], BF16)
    peers(depth, zed, lambda z: got(part_recv, z, r_part, s_part))
    total = part_own[zed]
    for z in range(depth):
        total = total + part_recv[z].astype(F32)

    def piece(q, c, z):
        return gathered.at[lax.div(q, 2), lax.rem(q, 2) * 2 + c, pl.ds(pl.multiple_of(z * span, span), span)]

    own = kind * 2 + lax.div(inner, 2)
    near = lax.div(group, 2) * 2
    gathered[kind, inner, pl.ds(pl.multiple_of(zed * span, span), span)] = total.astype(BF16)

    def same_core(q):
        return (zed * INNER + lax.rem(q, 2) * 2 + core, near + lax.div(q, 2))

    def send_z(z):
        here = piece(own, core, zed)
        copy(here, here, s_agz.at[z], r_agz.at[zed], at_depth(z)).start()
    peers(depth, zed, send_z)

    def to_sibling(q, z):
        here = piece(q, core, z)
        copy(here, here, s_agc.at[q, z], r_agc.at[q, z], sibling).start()

    def spread(z):
        here = piece(own, core, z)

        def send(q):
            copy(here, here, s_agp.at[q, z], r_agp.at[own, z], same_core(q)).start()
        peers(4, own, send)
        to_sibling(own, z)

    spread(zed)

    def take_z(z):
        here = piece(own, core, z)
        copy(here, here, s_agz.at[z], r_agz.at[z], (blk, group)).wait_recv()
        spread(z)
    peers(depth, zed, take_z)

    def relay(k, carry):
        z = lax.rem(zed + k, depth)

        def take(q):
            here = piece(q, core, z)
            copy(here, here, s_agp.at[q, z], r_agp.at[q, z], (blk, group)).wait_recv()
            to_sibling(q, z)
        peers(4, own, take)
        return carry
    lax.fori_loop(0, depth, relay, 0)

    def finish(k, carry):
        z = lax.rem(zed + k, depth)
        for q in range(4):
            there = piece(q, 1 - core, z)
            copy(there, there, s_agc.at[q, z], r_agc.at[q, z], sibling).wait_recv()
        return carry
    lax.fori_loop(0, depth, finish, 0)
    for p in range(4):
        audio_out[:, p * lanes:(p + 1) * lanes] = gathered[0, p]
        text_out[:, p * lanes:(p + 1) * lanes] = gathered[1, p]

    def sent(src, send, recv, at):
        copy(src, src, send.at[at], recv.at[at], (blk, group)).wait_send()

    def drain_half(q, carry):
        sent(clips.at[me], s_clipf, r_clip, q)
        sent(staged.at[0], s_featf, r_feat, q)
        return carry
    lax.fori_loop(0, half, drain_half, 0)

    def drain_same(q):
        sent(clips.at[me], s_clip, r_clip, q)
        sent(staged.at[0], s_feat, r_feat, q)
    peers(half, pos, drain_same)

    def drain_plane(a):
        sent(clip_send.at[a], s_cg, r_cg, a)
        sent(hid_send.at[0], s_hid, r_hid, a)
    peers(plane, me, drain_plane)

    def drain_depth(z):
        sent(texts.at[zed], s_text, r_text, z)
        sent(text_send.at[z], s_tg, r_tg, z)
        sent(part_send.at[z], s_part, r_part, z)
        sent(piece(own, core, zed), s_agz, r_agz, z)
    peers(depth, zed, drain_depth)

    def drain_out(z, carry):
        def one(q):
            here = piece(own, core, z)
            copy(here, here, s_agp.at[q, z], r_agp.at[q, z], (blk, group)).wait_send()
        peers(4, own, one)
        for q in range(4):
            here = piece(q, core, z)
            copy(here, here, s_agc.at[q, z], r_agc.at[q, z], sibling).wait_send()
        return carry
    lax.fori_loop(0, depth, drain_out, 0)


def per_device(blocks, groups, audio, audio_w, text, text_w, scale, bias):
    rows, wide = audio.shape
    width = audio_w.shape[1]
    depth, plane = blocks // INNER, INNER * groups
    lanes, span = width // 4, wide // depth
    vmem = pl.BlockSpec(memory_space=pltpu.VMEM)
    smem = pl.BlockSpec(memory_space=pltpu.SMEM)
    dma = pltpu.SemaphoreType.DMA
    half = plane // 2
    sems = [dma((count,)) for count in (
        4, half, half, plane, depth, depth, half, half, plane, plane, plane, depth, depth,
        plane, plane, depth, depth, depth, depth)]
    sems += [dma((4, depth))] * 4
    whole = jax.ShapeDtypeStruct((wide, width), BF16)
    hbm = pl.BlockSpec(memory_space=pl.ANY)
    grads = pl.pallas_call(
        functools.partial(kernel, blocks, groups),
        out_shape=(whole, whole),
        in_specs=[hbm, hbm, hbm, hbm, smem, smem],
        out_specs=(vmem, vmem),
        scratch_shapes=[
            pltpu.VMEM((plane, rows, width), BF16),
            pltpu.VMEM((depth, rows, width), BF16),
            pltpu.VMEM((2, rows, wide), BF16),
            pltpu.VMEM((2, wide, width), BF16),
            pltpu.VMEM((plane, rows, wide), BF16),
            pltpu.VMEM((plane, rows, depth * rows), BF16),
            pltpu.VMEM((plane, rows, width), BF16),
            pltpu.VMEM((plane, rows, width), BF16),
            pltpu.VMEM((depth, rows, width), BF16),
            pltpu.VMEM((depth, rows, width), BF16),
            pltpu.VMEM((rows, width), F32),
            pltpu.VMEM((rows, width), F32),
            pltpu.VMEM((2, rows, width), F32),
            pltpu.VMEM((2, rows, 128), F32),
            pltpu.VMEM((8, rows, lanes), F32),
            pltpu.VMEM((plane, rows, lanes), F32),
            pltpu.VMEM((depth, span, lanes), F32),
            pltpu.VMEM((depth, span, lanes), BF16),
            pltpu.VMEM((depth, span, lanes), BF16),
            pltpu.VMEM((2, 4, wide, lanes), BF16),
        ] + sems,
        compiler_params=pltpu.CompilerParams(
            collective_id=0, has_side_effects=True, vmem_limit_bytes=56 * 1024 * 1024),
    )(audio, audio_w, text, text_w, scale, bias)
    return tuple(grad.astype(F32) for grad in grads)


def solution(mesh):
    placed = (P(("blk", "group"), None), P(), P(("blk", "group"), None), P(), P(), P())
    step = functools.partial(per_device, mesh.shape["blk"], mesh.shape["group"])
    return jax.shard_map(step, mesh=mesh, in_specs=placed, out_specs=(P(), P()), check_vma=False)
```

```python
import functools

import jax
import jax.numpy as jnp
from jax import lax
from jax.experimental import pallas as pl
from jax.experimental.pallas import tpu as pltpu
from jax.sharding import PartitionSpec as P

EPSILON = 1e-06
BF16 = jnp.bfloat16
F32 = jnp.float32
INNER = 4
TN = (((0,), (0,)), ((), ()))
NT = (((1,), (1,)), ((), ()))


def kernel(
    blocks, groups,
    audio_ref, audio_w_ref, text_ref, text_w_ref, scale_ref, bias_ref,
    audio_out, text_out,
    clips, texts, staged, weights, feats, gates, clip_give, clip_take, clip_send, clip_recv, text_send, text_recv,
    clip_own, text_own, units, norms, hid_send, hid_recv, part_own, part_send, part_recv, gathered,
    s_in, s_clip, s_clipf, r_clip, s_text, r_text, s_feat, s_featf, r_feat, s_give, r_give, s_cg, r_cg, s_tg, r_tg,
    s_hid, r_hid, s_part, r_part, s_agz, r_agz, s_agp, r_agp, s_agc, r_agc,
):
    depth = blocks // INNER
    plane = INNER * groups
    rows = audio_ref.shape[0]
    width = audio_w_ref.shape[1]
    lanes = width // 4
    span = audio_w_ref.shape[0] // depth
    blk = lax.axis_index("blk")
    group = lax.axis_index("group")
    zed = lax.div(blk, INNER)
    inner = lax.rem(blk, INNER)
    me = inner * groups + group

    def at_plane(a):
        return (zed * INNER + lax.div(a, groups), lax.rem(a, groups))

    def at_depth(z):
        return (z * INNER + inner, group)

    half = plane // 2
    core = lax.rem(inner, 2)
    pos = lax.div(inner, 2) * groups + group
    sibling = (zed * INNER + inner + 1 - 2 * core, group)

    def block_at(q, c):
        return (lax.div(q, groups) * 2 + c) * groups + lax.rem(q, groups)

    def kind_of(a):
        return lax.rem(lax.rem(a, groups), 2)

    def role(a):
        return kind_of(a) * 4 + lax.div(a, groups)

    sources = (audio_ref, text_ref, audio_w_ref, text_w_ref)
    targets = (staged.at[0], staged.at[1], weights.at[0], weights.at[1])
    loads = [pltpu.make_async_copy(sources[k], targets[k], s_in.at[k]) for k in range(4)]
    for k in (1, 3, 0, 2):
        loads[k].start()

    def copy(src, dst, send, recv, device):
        return pltpu.make_async_remote_copy(
            src_ref=src, dst_ref=dst, send_sem=send, recv_sem=recv,
            device_id=device, device_id_type=pl.DeviceIdType.MESH,
        )

    def peers(count, own, fn):
        def body(k, carry):
            fn(lax.rem(own + k, count))
            return carry
        lax.fori_loop(1, count, body, 0)

    mine = role(me)
    kind = kind_of(me)

    barrier = pltpu.get_barrier_semaphore()
    peers(plane, me, lambda a: pl.semaphore_signal(
        barrier, inc=1, device_id=at_plane(a), device_id_type=pl.DeviceIdType.MESH))
    peers(depth, zed, lambda z: pl.semaphore_signal(
        barrier, inc=1, device_id=at_depth(z), device_id_type=pl.DeviceIdType.MESH))

    def embed(at):
        hidden = jnp.dot(staged[at], weights[at], preferred_element_type=F32)
        norm = jnp.sqrt(jnp.sum(hidden * hidden, axis=1, keepdims=True) + EPSILON)
        unit = hidden / norm
        units[at] = unit
        norms[at] = jnp.broadcast_to(norm, (rows, 128))
        return unit.astype(BF16)

    loads[1].wait()
    loads[3].wait()
    texts[zed] = embed(1)
    pl.semaphore_wait(barrier, plane - 1 + depth - 1)

    def send_text(z):
        copy(texts.at[zed], texts.at[zed], s_text.at[z], r_text.at[zed], at_depth(z)).start()
    peers(depth, zed, send_text)

    loads[0].wait()
    loads[2].wait()
    clips[me] = embed(0)

    def send_clip(q):
        copy(clips.at[me], clips.at[me], s_clip.at[q], r_clip.at[me], at_plane(block_at(q, core))).start()
    peers(half, pos, send_clip)
    copy(clips.at[me], clips.at[me], s_clipf.at[pos], r_clip.at[me], sibling).start()

    feats[me] = staged[kind]

    def send_feat(q):
        a = block_at(q, core)
        copy(staged.at[kind_of(a)], feats.at[me], s_feat.at[q], r_feat.at[me], at_plane(a)).start()
    peers(half, pos, send_feat)
    copy(staged.at[kind], feats.at[me], s_featf.at[pos], r_feat.at[me], sibling).start()

    def got(buf, at, recv, send):
        copy(buf.at[at], buf.at[at], send.at[0], recv.at[at], (blk, group)).wait_recv()

    def pass_clip(q):
        a = block_at(q, core)
        got(clips, a, r_clip, s_clip)
        copy(clips.at[a], clips.at[a], s_clipf.at[q], r_clip.at[a], sibling).start()
    peers(half, pos, pass_clip)

    def take_clip(q, carry):
        got(clips, block_at(q, 1 - core), r_clip, s_clip)
        return carry
    lax.fori_loop(0, half, take_clip, 0)

    scale = scale_ref[0]
    bias = bias_ref[0]

    def all_clips():
        return clips[...].reshape(plane * rows, width)

    def columns(z):
        return pl.ds(pl.multiple_of(z * rows, rows), rows)

    def logits_of(z):
        return scale * lax.dot_general(all_clips(), texts[z], NT, preferred_element_type=F32) + bias

    def text_term(gate):
        return lax.dot_general(gate, all_clips(), TN, preferred_element_type=F32)

    logits = logits_of(zed)
    row = lax.broadcasted_iota(jnp.int32, logits.shape, 0)
    column = lax.broadcasted_iota(jnp.int32, logits.shape, 1)
    sign = jnp.where(row - column == me * rows, 1.0, -1.0)
    own_gate = (-sign / (1.0 + jnp.exp(sign * logits))).astype(BF16)
    gates[:, :, columns(zed)] = own_gate.reshape(plane, rows, rows)

    def text_step(z):
        got(texts, z, r_text, s_text)
        gate = (1.0 / (1.0 + jnp.exp(-logits_of(z)))).astype(BF16)
        text_send[z] = text_term(gate).astype(BF16)
        copy(text_send.at[z], text_recv.at[zed], s_tg.at[z], r_tg.at[zed], at_depth(z)).start()
        gates[:, :, columns(z)] = gate.reshape(plane, rows, rows)
    peers(depth, zed, text_step)

    def clip_term(a):
        return jnp.dot(gates[a], texts[...].reshape(depth * rows, width), preferred_element_type=F32)

    def give_clip(q, carry):
        clip_give[q] = clip_term(block_at(q, 1 - core)).astype(BF16)
        copy(clip_give.at[q], clip_take.at[q], s_give.at[q], r_give.at[q], sibling).start()
        return carry
    lax.fori_loop(0, half, give_clip, 0)

    def send_sum(q):
        term = clip_term(block_at(q, core))
        got(clip_take, q, r_give, s_give)
        clip_send[q] = (term + clip_take[q].astype(F32)).astype(BF16)
        copy(clip_send.at[q], clip_recv.at[pos], s_cg.at[q], r_cg.at[pos], at_plane(block_at(q, core))).start()
    peers(half, pos, send_sum)
    own_term = clip_term(me)
    got(clip_take, pos, r_give, s_give)
    clip_own[...] = own_term + clip_take[pos].astype(F32)

    def pass_feat(q):
        a = block_at(q, core)
        got(feats, a, r_feat, s_feat)
        copy(feats.at[a], feats.at[a], s_featf.at[q], r_feat.at[a], sibling).start()
    peers(half, pos, pass_feat)

    text_own[...] = text_term(gates[:, :, columns(zed)].reshape(plane * rows, rows))

    def backward(at, own, grad):
        unit = units[at]
        grad = scale * grad
        inner_sum = jnp.sum(unit * grad, axis=1, keepdims=True)
        result = (grad - unit * inner_sum) / norms[at][:, :1]
        for s in range(4):
            hid_send[4 * at + s] = result[:, s * lanes:(s + 1) * lanes]

    def add_clip(a):
        got(clip_recv, a, r_cg, s_cg)
        clip_own[...] += clip_recv[a].astype(F32)
    peers(half, pos, add_clip)
    backward(0, clip_own, clip_own[...])

    def send_hid(want, a):
        @pl.when(kind_of(a) == want)
        def _():
            copy(hid_send.at[role(a)], hid_recv.at[me], s_hid.at[a], r_hid.at[me], at_plane(a)).start()
    peers(plane, me, functools.partial(send_hid, 0))

    def add_text(z):
        got(text_recv, z, r_tg, s_tg)
        text_own[...] += text_recv[z].astype(F32)
    peers(depth, zed, add_text)
    backward(1, text_own, text_own[...])
    peers(plane, me, functools.partial(send_hid, 1))
    hid_recv[me] = hid_send[mine]

    def take_feat(q, carry):
        got(feats, block_at(q, 1 - core), r_feat, s_feat)
        return carry
    lax.fori_loop(0, half, take_feat, 0)
    peers(plane, me, lambda a: got(hid_recv, a, r_hid, s_hid))
    hidden = hid_recv[...].reshape(plane * rows, lanes)
    high = hidden.astype(BF16)
    low = (hidden - high.astype(F32)).astype(BF16)
    both = lax.dot_general(
        feats[...].reshape(plane * rows, feats.shape[2]),
        jnp.concatenate([high, low], axis=1), TN, preferred_element_type=F32)
    terms = (both[:, :lanes] + both[:, lanes:]).reshape(part_own.shape)
    part_own[...] = terms
    part_send[...] = terms.astype(BF16)

    def send_part(z):
        copy(part_send.at[z], part_recv.at[zed], s_part.at[z], r_part.at[zed], at_depth(z)).start()
    peers(depth, zed, send_part)
    part_recv[zed] = jnp.zeros(part_recv.shape[1:], BF16)
    peers(depth, zed, lambda z: got(part_recv, z, r_part, s_part))
    total = part_own[zed]
    for z in range(depth):
        total = total + part_recv[z].astype(F32)

    def piece(q, c, z):
        return gathered.at[lax.div(q, 2), lax.rem(q, 2) * 2 + c, pl.ds(pl.multiple_of(z * span, span), span)]

    own = kind * 2 + lax.div(inner, 2)
    near = lax.div(group, 2) * 2
    gathered[kind, inner, pl.ds(pl.multiple_of(zed * span, span), span)] = total.astype(BF16)

    def same_core(q):
        return (zed * INNER + lax.rem(q, 2) * 2 + core, near + lax.div(q, 2))

    def send_z(z):
        here = piece(own, core, zed)
        copy(here, here, s_agz.at[z], r_agz.at[zed], at_depth(z)).start()
    peers(depth, zed, send_z)

    def to_sibling(q, z):
        here = piece(q, core, z)
        copy(here, here, s_agc.at[q, z], r_agc.at[q, z], sibling).start()

    def spread(z):
        here = piece(own, core, z)

        def send(q):
            copy(here, here, s_agp.at[q, z], r_agp.at[own, z], same_core(q)).start()
        peers(4, own, send)
        to_sibling(own, z)

    spread(zed)

    def take_z(z):
        here = piece(own, core, z)
        copy(here, here, s_agz.at[z], r_agz.at[z], (blk, group)).wait_recv()
        spread(z)
    peers(depth, zed, take_z)

    def relay(k, carry):
        z = lax.rem(zed + k, depth)

        def take(q):
            here = piece(q, core, z)
            copy(here, here, s_agp.at[q, z], r_agp.at[q, z], (blk, group)).wait_recv()
            to_sibling(q, z)
        peers(4, own, take)
        return carry
    lax.fori_loop(0, depth, relay, 0)

    def finish(k, carry):
        z = lax.rem(zed + k, depth)
        for q in range(4):
            there = piece(q, 1 - core, z)
            copy(there, there, s_agc.at[q, z], r_agc.at[q, z], sibling).wait_recv()
        return carry
    lax.fori_loop(0, depth, finish, 0)
    for p in range(4):
        audio_out[:, p * lanes:(p + 1) * lanes] = gathered[0, p]
        text_out[:, p * lanes:(p + 1) * lanes] = gathered[1, p]

    def sent(src, send, recv, at):
        copy(src, src, send.at[at], recv.at[at], (blk, group)).wait_send()

    def drain_half(q, carry):
        sent(clips.at[me], s_clipf, r_clip, q)
        sent(staged.at[0], s_featf, r_feat, q)
        sent(clip_give.at[q], s_give, r_give, q)
        return carry
    lax.fori_loop(0, half, drain_half, 0)

    def drain_same(q):
        sent(clips.at[me], s_clip, r_clip, q)
        sent(staged.at[0], s_feat, r_feat, q)
        sent(clip_send.at[q], s_cg, r_cg, q)
    peers(half, pos, drain_same)

    def drain_plane(a):
        sent(hid_send.at[0], s_hid, r_hid, a)
    peers(plane, me, drain_plane)

    def drain_depth(z):
        sent(texts.at[zed], s_text, r_text, z)
        sent(text_send.at[z], s_tg, r_tg, z)
        sent(part_send.at[z], s_part, r_part, z)
        sent(piece(own, core, zed), s_agz, r_agz, z)
    peers(depth, zed, drain_depth)

    def drain_out(z, carry):
        def one(q):
            here = piece(own, core, z)
            copy(here, here, s_agp.at[q, z], r_agp.at[q, z], (blk, group)).wait_send()
        peers(4, own, one)
        for q in range(4):
            here = piece(q, core, z)
            copy(here, here, s_agc.at[q, z], r_agc.at[q, z], sibling).wait_send()
        return carry
    lax.fori_loop(0, depth, drain_out, 0)


def per_device(blocks, groups, audio, audio_w, text, text_w, scale, bias):
    rows, wide = audio.shape
    width = audio_w.shape[1]
    depth, plane = blocks // INNER, INNER * groups
    lanes, span = width // 4, wide // depth
    vmem = pl.BlockSpec(memory_space=pltpu.VMEM)
    smem = pl.BlockSpec(memory_space=pltpu.SMEM)
    dma = pltpu.SemaphoreType.DMA
    half = plane // 2
    sems = [dma((count,)) for count in (
        4, half, half, plane, depth, depth, half, half, plane, half, half, half, half, depth, depth,
        plane, plane, depth, depth, depth, depth)]
    sems += [dma((4, depth))] * 4
    whole = jax.ShapeDtypeStruct((wide, width), BF16)
    hbm = pl.BlockSpec(memory_space=pl.ANY)
    grads = pl.pallas_call(
        functools.partial(kernel, blocks, groups),
        out_shape=(whole, whole),
        in_specs=[hbm, hbm, hbm, hbm, smem, smem],
        out_specs=(vmem, vmem),
        scratch_shapes=[
            pltpu.VMEM((plane, rows, width), BF16),
            pltpu.VMEM((depth, rows, width), BF16),
            pltpu.VMEM((2, rows, wide), BF16),
            pltpu.VMEM((2, wide, width), BF16),
            pltpu.VMEM((plane, rows, wide), BF16),
            pltpu.VMEM((plane, rows, depth * rows), BF16),
            pltpu.VMEM((half, rows, width), BF16),
            pltpu.VMEM((half, rows, width), BF16),
            pltpu.VMEM((half, rows, width), BF16),
            pltpu.VMEM((half, rows, width), BF16),
            pltpu.VMEM((depth, rows, width), BF16),
            pltpu.VMEM((depth, rows, width), BF16),
            pltpu.VMEM((rows, width), F32),
            pltpu.VMEM((rows, width), F32),
            pltpu.VMEM((2, rows, width), F32),
            pltpu.VMEM((2, rows, 128), F32),
            pltpu.VMEM((8, rows, lanes), F32),
            pltpu.VMEM((plane, rows, lanes), F32),
            pltpu.VMEM((depth, span, lanes), F32),
            pltpu.VMEM((depth, span, lanes), BF16),
            pltpu.VMEM((depth, span, lanes), BF16),
            pltpu.VMEM((2, 4, wide, lanes), BF16),
        ] + sems,
        compiler_params=pltpu.CompilerParams(
            collective_id=0, has_side_effects=True, vmem_limit_bytes=56 * 1024 * 1024),
    )(audio, audio_w, text, text_w, scale, bias)
    return tuple(grad.astype(F32) for grad in grads)


def solution(mesh):
    placed = (P(("blk", "group"), None), P(), P(("blk", "group"), None), P(), P(), P())
    step = functools.partial(per_device, mesh.shape["blk"], mesh.shape["group"])
    return jax.shard_map(step, mesh=mesh, in_specs=placed, out_specs=(P(), P()), check_vma=False)
```

```python
import functools

import jax
import jax.numpy as jnp
from jax import lax
from jax.experimental import pallas as pl
from jax.experimental.pallas import tpu as pltpu
from jax.sharding import PartitionSpec as P

EPSILON = 1e-06
BF16 = jnp.bfloat16
F32 = jnp.float32
INNER = 4
TN = (((0,), (0,)), ((), ()))
NT = (((1,), (1,)), ((), ()))


def kernel(
    blocks, groups,
    audio_ref, audio_w_ref, text_ref, text_w_ref, scale_ref, bias_ref,
    out,
    clips, texts, staged, weights, feats, gates, clip_give, clip_take, clip_send, clip_recv, text_send, text_recv,
    clip_own, text_own, units, norms, hid_send, hid_recv, part_own, part_send, part_recv, gathered,
    s_in, s_clip, s_clipf, r_clip, s_text, r_text, s_feat, s_featf, r_feat, s_give, r_give, s_cg, r_cg, s_tg, r_tg,
    s_hid, r_hid, s_part, r_part, s_agz, r_agz, s_agp, r_agp, s_agc, r_agc,
):
    depth = blocks // INNER
    plane = INNER * groups
    rows = audio_ref.shape[0]
    width = audio_w_ref.shape[1]
    lanes = width // 4
    span = audio_w_ref.shape[0] // depth
    blk = lax.axis_index("blk")
    group = lax.axis_index("group")
    zed = lax.div(blk, INNER)
    inner = lax.rem(blk, INNER)
    me = inner * groups + group

    def at_plane(a):
        return (zed * INNER + lax.div(a, groups), lax.rem(a, groups))

    def at_depth(z):
        return (z * INNER + inner, group)

    half = plane // 2
    core = lax.rem(inner, 2)
    pos = lax.div(inner, 2) * groups + group
    sibling = (zed * INNER + inner + 1 - 2 * core, group)

    def block_at(q, c):
        return (lax.div(q, groups) * 2 + c) * groups + lax.rem(q, groups)

    def kind_of(a):
        return lax.rem(lax.rem(a, groups), 2)

    def role(a):
        return kind_of(a) * 4 + lax.div(a, groups)

    sources = (audio_ref, text_ref, audio_w_ref, text_w_ref)
    targets = (staged.at[0], staged.at[1], weights.at[0], weights.at[1])
    loads = [pltpu.make_async_copy(sources[k], targets[k], s_in.at[k]) for k in range(4)]
    for k in (1, 3, 0, 2):
        loads[k].start()

    def copy(src, dst, send, recv, device):
        return pltpu.make_async_remote_copy(
            src_ref=src, dst_ref=dst, send_sem=send, recv_sem=recv,
            device_id=device, device_id_type=pl.DeviceIdType.MESH,
        )

    def peers(count, own, fn):
        def body(k, carry):
            fn(lax.rem(own + k, count))
            return carry
        lax.fori_loop(1, count, body, 0)

    mine = role(me)
    kind = kind_of(me)

    barrier = pltpu.get_barrier_semaphore()
    peers(plane, me, lambda a: pl.semaphore_signal(
        barrier, inc=1, device_id=at_plane(a), device_id_type=pl.DeviceIdType.MESH))
    peers(depth, zed, lambda z: pl.semaphore_signal(
        barrier, inc=1, device_id=at_depth(z), device_id_type=pl.DeviceIdType.MESH))

    def embed(at):
        hidden = jnp.dot(staged[at], weights[at], preferred_element_type=F32)
        norm = jnp.sqrt(jnp.sum(hidden * hidden, axis=1, keepdims=True) + EPSILON)
        unit = hidden / norm
        units[at] = unit
        norms[at] = jnp.broadcast_to(norm, (rows, 128))
        return unit.astype(BF16)

    loads[1].wait()
    loads[3].wait()
    texts[zed] = embed(1)
    loads[0].wait()
    loads[2].wait()
    clips[me] = embed(0)
    feats[me] = staged[kind]
    pl.semaphore_wait(barrier, plane - 1 + depth - 1)

    def send_text(z):
        copy(texts.at[zed], texts.at[zed], s_text.at[z], r_text.at[zed], at_depth(z)).start()
    peers(depth, zed, send_text)

    def send_clip(q):
        copy(clips.at[me], clips.at[me], s_clip.at[q], r_clip.at[me], at_plane(block_at(q, core))).start()
    peers(half, pos, send_clip)
    copy(clips.at[me], clips.at[me], s_clipf.at[pos], r_clip.at[me], sibling).start()

    def send_feat(q):
        a = block_at(q, core)
        copy(staged.at[kind_of(a)], feats.at[me], s_feat.at[q], r_feat.at[me], at_plane(a)).start()
    peers(half, pos, send_feat)
    copy(staged.at[kind], feats.at[me], s_featf.at[pos], r_feat.at[me], sibling).start()

    def got(buf, at, recv, send):
        copy(buf.at[at], buf.at[at], send.at[0], recv.at[at], (blk, group)).wait_recv()

    def pass_clip(q):
        a = block_at(q, core)
        got(clips, a, r_clip, s_clip)
        copy(clips.at[a], clips.at[a], s_clipf.at[q], r_clip.at[a], sibling).start()
    peers(half, pos, pass_clip)

    def take_clip(q, carry):
        got(clips, block_at(q, 1 - core), r_clip, s_clip)
        return carry
    lax.fori_loop(0, half, take_clip, 0)

    scale = scale_ref[0]
    bias = bias_ref[0]

    def all_clips():
        return clips[...].reshape(plane * rows, width)

    def columns(z):
        return pl.ds(pl.multiple_of(z * rows, rows), rows)

    def logits_of(z):
        return scale * lax.dot_general(all_clips(), texts[z], NT, preferred_element_type=F32) + bias

    def text_term(gate):
        return lax.dot_general(gate, all_clips(), TN, preferred_element_type=F32)

    logits = logits_of(zed)
    row = lax.broadcasted_iota(jnp.int32, logits.shape, 0)
    column = lax.broadcasted_iota(jnp.int32, logits.shape, 1)
    sign = jnp.where(row - column == me * rows, 1.0, -1.0)
    own_gate = (-sign / (1.0 + jnp.exp(sign * logits))).astype(BF16)
    gates[:, :, columns(zed)] = own_gate.reshape(plane, rows, rows)

    def text_step(z):
        got(texts, z, r_text, s_text)
        gate = (1.0 / (1.0 + jnp.exp(-logits_of(z)))).astype(BF16)
        text_send[z] = text_term(gate).astype(BF16)
        copy(text_send.at[z], text_recv.at[zed], s_tg.at[z], r_tg.at[zed], at_depth(z)).start()
        gates[:, :, columns(z)] = gate.reshape(plane, rows, rows)
    peers(depth, zed, text_step)

    def clip_term(a):
        return jnp.dot(gates[a], texts[...].reshape(depth * rows, width), preferred_element_type=F32)

    def give_clip(q, carry):
        clip_give[q] = clip_term(block_at(q, 1 - core)).astype(BF16)
        copy(clip_give.at[q], clip_take.at[q], s_give.at[q], r_give.at[q], sibling).start()
        return carry
    lax.fori_loop(0, half, give_clip, 0)

    def send_sum(q):
        term = clip_term(block_at(q, core))
        got(clip_take, q, r_give, s_give)
        clip_send[q] = (term + clip_take[q].astype(F32)).astype(BF16)
        copy(clip_send.at[q], clip_recv.at[pos], s_cg.at[q], r_cg.at[pos], at_plane(block_at(q, core))).start()
    peers(half, pos, send_sum)
    own_term = clip_term(me)
    got(clip_take, pos, r_give, s_give)
    clip_own[...] = own_term + clip_take[pos].astype(F32)

    def pass_feat(q):
        a = block_at(q, core)
        got(feats, a, r_feat, s_feat)
        copy(feats.at[a], feats.at[a], s_featf.at[q], r_feat.at[a], sibling).start()
    peers(half, pos, pass_feat)

    text_own[...] = text_term(gates[:, :, columns(zed)].reshape(plane * rows, rows))

    def backward(at, own, grad):
        unit = units[at]
        grad = scale * grad
        inner_sum = jnp.sum(unit * grad, axis=1, keepdims=True)
        result = (grad - unit * inner_sum) / norms[at][:, :1]
        for s in range(4):
            hid_send[4 * at + s] = result[:, s * lanes:(s + 1) * lanes]

    def add_clip(a):
        got(clip_recv, a, r_cg, s_cg)
        clip_own[...] += clip_recv[a].astype(F32)
    peers(half, pos, add_clip)
    backward(0, clip_own, clip_own[...])

    def send_hid(want, a):
        @pl.when(kind_of(a) == want)
        def _():
            copy(hid_send.at[role(a)], hid_recv.at[me], s_hid.at[a], r_hid.at[me], at_plane(a)).start()
    peers(plane, me, functools.partial(send_hid, 0))

    def add_text(z):
        got(text_recv, z, r_tg, s_tg)
        text_own[...] += text_recv[z].astype(F32)
    peers(depth, zed, add_text)
    backward(1, text_own, text_own[...])
    peers(plane, me, functools.partial(send_hid, 1))
    hid_recv[me] = hid_send[mine]

    def take_feat(q, carry):
        got(feats, block_at(q, 1 - core), r_feat, s_feat)
        return carry
    lax.fori_loop(0, half, take_feat, 0)
    peers(plane, me, lambda a: got(hid_recv, a, r_hid, s_hid))
    hidden = hid_recv[...].reshape(plane * rows, lanes)
    high = hidden.astype(BF16)
    low = (hidden - high.astype(F32)).astype(BF16)
    both = lax.dot_general(
        feats[...].reshape(plane * rows, feats.shape[2]),
        jnp.concatenate([high, low], axis=1), TN, preferred_element_type=F32)
    terms = (both[:, :lanes] + both[:, lanes:]).reshape(part_own.shape)
    part_own[...] = terms
    part_send[...] = terms.astype(BF16)

    def send_part(z):
        copy(part_send.at[z], part_recv.at[zed], s_part.at[z], r_part.at[zed], at_depth(z)).start()
    peers(depth, zed, send_part)
    part_recv[zed] = jnp.zeros(part_recv.shape[1:], BF16)

    def sent(src, send, recv, at):
        copy(src, src, send.at[at], recv.at[0], (blk, group)).wait_send()

    def drain_half(q, carry):
        sent(clips.at[me], s_clipf, r_clip, q)
        sent(staged.at[0], s_featf, r_feat, q)
        sent(clip_give.at[q], s_give, r_give, q)
        return carry
    lax.fori_loop(0, half, drain_half, 0)

    def drain_same(q):
        sent(clips.at[me], s_clip, r_clip, q)
        sent(staged.at[0], s_feat, r_feat, q)
        sent(clip_send.at[q], s_cg, r_cg, q)
    peers(half, pos, drain_same)
    peers(plane, me, lambda a: sent(hid_send.at[0], s_hid, r_hid, a))

    def drain_depth(z):
        sent(texts.at[zed], s_text, r_text, z)
        sent(text_send.at[z], s_tg, r_tg, z)
    peers(depth, zed, drain_depth)

    peers(depth, zed, lambda z: got(part_recv, z, r_part, s_part))
    total = part_own[zed]
    for z in range(depth):
        total = total + part_recv[z].astype(F32)

    def rows_of(z):
        return pl.ds(pl.multiple_of(z * span, span), span)

    own = kind * 2 + lax.div(inner, 2)
    near = lax.div(group, 2) * 2
    gathered[core, own, rows_of(zed)] = total.astype(BF16)

    def same_core(q):
        return (zed * INNER + lax.rem(q, 2) * 2 + core, near + lax.div(q, 2))

    def spread(z):
        here = gathered.at[core, own, rows_of(z)]
        peers(4, own, lambda q: copy(here, here, s_agp.at[0], r_agp.at[z], same_core(q)).start())

    def send_z(z):
        here = gathered.at[core, own, rows_of(zed)]
        copy(here, here, s_agz.at[z], r_agz.at[zed], at_depth(z)).start()
    peers(depth, zed, send_z)
    spread(zed)

    def take_z(z):
        here = gathered.at[core, own, rows_of(z)]
        copy(here, here, s_agz.at[z], r_agz.at[z], (blk, group)).wait_recv()
        spread(z)
    peers(depth, zed, take_z)

    def relay(k, carry):
        z = lax.rem(zed + k, depth)
        three = gathered.at[core, pl.ds(0, 3), rows_of(z)]
        copy(three, three, s_agp.at[0], r_agp.at[z], (blk, group)).wait_recv()
        here = gathered.at[core, :, rows_of(z)]
        copy(here, here, s_agc.at[z], r_agc.at[z], sibling).start()
        return carry
    lax.fori_loop(0, depth, relay, 0)

    def place(c):
        for q in range(4):
            at = pl.multiple_of(((q % 2) * 2 + c) * lanes, lanes)
            out[q // 2, :, pl.ds(at, lanes)] = gathered[c, q]
    place(core)

    def finish(k, carry):
        z = lax.rem(zed + k, depth)
        there = gathered.at[1 - core, :, rows_of(z)]
        copy(there, there, s_agc.at[z], r_agc.at[z], sibling).wait_recv()
        return carry
    lax.fori_loop(0, depth, finish, 0)
    place(1 - core)

    def drain_out(z):
        sent(part_send.at[z], s_part, r_part, z)
        sent(gathered.at[core, own, rows_of(zed)], s_agz, r_agz, z)
    peers(depth, zed, drain_out)
    sent(gathered.at[core, pl.ds(0, 3)], s_agp, r_agp, 0)

    def drain_relay(z, carry):
        sent(gathered.at[core, :, rows_of(z)], s_agc, r_agc, z)
        return carry
    lax.fori_loop(0, depth, drain_relay, 0)


def per_device(blocks, groups, audio, audio_w, text, text_w, scale, bias):
    rows, wide = audio.shape
    width = audio_w.shape[1]
    depth, plane = blocks // INNER, INNER * groups
    lanes, span = width // 4, wide // depth
    vmem = pl.BlockSpec(memory_space=pltpu.VMEM)
    smem = pl.BlockSpec(memory_space=pltpu.SMEM)
    dma = pltpu.SemaphoreType.DMA
    half = plane // 2
    sems = [dma((count,)) for count in (
        4, half, half, plane, depth, depth, half, half, plane, half, half, half, half, depth, depth,
        plane, plane, depth, depth, depth, depth)]
    sems += [dma((count,)) for count in (1, depth, depth, depth)]
    whole = jax.ShapeDtypeStruct((2, wide, width), BF16)
    hbm = pl.BlockSpec(memory_space=pl.ANY)
    grads = pl.pallas_call(
        functools.partial(kernel, blocks, groups),
        out_shape=whole,
        in_specs=[hbm, hbm, hbm, hbm, smem, smem],
        out_specs=vmem,
        scratch_shapes=[
            pltpu.VMEM((plane, rows, width), BF16),
            pltpu.VMEM((depth, rows, width), BF16),
            pltpu.VMEM((2, rows, wide), BF16),
            pltpu.VMEM((2, wide, width), BF16),
            pltpu.VMEM((plane, rows, wide), BF16),
            pltpu.VMEM((plane, rows, depth * rows), BF16),
            pltpu.VMEM((half, rows, width), BF16),
            pltpu.VMEM((half, rows, width), BF16),
            pltpu.VMEM((half, rows, width), BF16),
            pltpu.VMEM((half, rows, width), BF16),
            pltpu.VMEM((depth, rows, width), BF16),
            pltpu.VMEM((depth, rows, width), BF16),
            pltpu.VMEM((rows, width), F32),
            pltpu.VMEM((rows, width), F32),
            pltpu.VMEM((2, rows, width), F32),
            pltpu.VMEM((2, rows, 128), F32),
            pltpu.VMEM((8, rows, lanes), F32),
            pltpu.VMEM((plane, rows, lanes), F32),
            pltpu.VMEM((depth, span, lanes), F32),
            pltpu.VMEM((depth, span, lanes), BF16),
            pltpu.VMEM((depth, span, lanes), BF16),
            pltpu.VMEM((2, 4, wide, lanes), BF16),
        ] + sems,
        compiler_params=pltpu.CompilerParams(
            collective_id=0, has_side_effects=True, vmem_limit_bytes=56 * 1024 * 1024),
    )(audio, audio_w, text, text_w, scale, bias)
    return grads[0].astype(F32), grads[1].astype(F32)


def solution(mesh):
    placed = (P(("blk", "group"), None), P(), P(("blk", "group"), None), P(), P(), P())
    step = functools.partial(per_device, mesh.shape["blk"], mesh.shape["group"])
    return jax.shard_map(step, mesh=mesh, in_specs=placed, out_specs=(P(), P()), check_vma=False)
```

```python
import functools

import jax
import jax.numpy as jnp
from jax import lax
from jax.experimental import pallas as pl
from jax.experimental.pallas import tpu as pltpu
from jax.sharding import PartitionSpec as P

EPSILON = 1e-06
BF16 = jnp.bfloat16
F32 = jnp.float32
INNER = 4
TN = (((0,), (0,)), ((), ()))
NT = (((1,), (1,)), ((), ()))


def kernel(
    blocks, groups,
    audio_ref, audio_w_ref, text_ref, text_w_ref, scale_ref, bias_ref,
    out,
    clips, texts, staged, weights, feats, gates, clip_give, clip_take, clip_send, clip_recv, text_send, text_recv,
    clip_own, text_own, units, norms, hid_send, hid_recv, part_own, part_send, part_recv, gathered,
    s_in, s_clip, s_clipf, r_clip, s_text, s_textd, r_text, s_feat, s_featf, r_feat, s_give, r_give, s_cg, r_cg, s_tg, r_tg,
    s_hid, r_hid, s_part, r_part, s_agz, s_agzd, r_agz, s_agp, r_agp, s_agc, r_agc,
):
    depth = blocks // INNER
    plane = INNER * groups
    rows = audio_ref.shape[0]
    width = audio_w_ref.shape[1]
    lanes = width // 4
    span = audio_w_ref.shape[0] // depth
    blk = lax.axis_index("blk")
    group = lax.axis_index("group")
    zed = lax.div(blk, INNER)
    inner = lax.rem(blk, INNER)
    me = inner * groups + group

    def at_plane(a):
        return (zed * INNER + lax.div(a, groups), lax.rem(a, groups))

    def at_depth(z):
        return (z * INNER + inner, group)

    half = plane // 2
    core = lax.rem(inner, 2)
    pos = lax.div(inner, 2) * groups + group
    sibling = (zed * INNER + inner + 1 - 2 * core, group)

    def block_at(q, c):
        return (lax.div(q, groups) * 2 + c) * groups + lax.rem(q, groups)

    def kind_of(a):
        return lax.rem(lax.rem(a, groups), 2)

    def role(a):
        return kind_of(a) * 4 + lax.div(a, groups)

    sources = (audio_ref, text_ref, audio_w_ref, text_w_ref)
    targets = (staged.at[0], staged.at[1], weights.at[0], weights.at[1])
    loads = [pltpu.make_async_copy(sources[k], targets[k], s_in.at[k]) for k in range(4)]
    for k in (1, 3, 0, 2):
        loads[k].start()

    def copy(src, dst, send, recv, device):
        return pltpu.make_async_remote_copy(
            src_ref=src, dst_ref=dst, send_sem=send, recv_sem=recv,
            device_id=device, device_id_type=pl.DeviceIdType.MESH,
        )

    def peers(count, own, fn):
        def body(k, carry):
            fn(lax.rem(own + k, count))
            return carry
        lax.fori_loop(1, count, body, 0)

    def nearest(fn, low, high):
        def body(d, carry):
            pl.when(zed >= d)(lambda: fn(zed - d))
            pl.when(zed + d < depth)(lambda: fn(zed + d))
            return carry
        lax.fori_loop(low, high, body, 0)

    class Chain:
        def __init__(self, block, up, down, recv):
            self.block, self.up, self.down, self.recv = block, up, down, recv

        def forward(self, b):
            here = self.block(b)

            @pl.when(jnp.logical_and(b <= zed, zed + 1 < depth))
            def _():
                copy(here, here, self.up.at[b], self.recv.at[b], at_depth(zed + 1)).start()

            @pl.when(jnp.logical_and(b >= zed, zed > 0))
            def _():
                copy(here, here, self.down.at[b], self.recv.at[b], at_depth(zed - 1)).start()

        def take(self, b):
            here = self.block(b)
            copy(here, here, self.up.at[b], self.recv.at[b], (blk, group)).wait_recv()
            self.forward(b)

        def drain(self):
            def body(b, carry):
                here = self.block(b)

                @pl.when(jnp.logical_and(b <= zed, zed + 1 < depth))
                def _():
                    copy(here, here, self.up.at[b], self.recv.at[b], (blk, group)).wait_send()

                @pl.when(jnp.logical_and(b >= zed, zed > 0))
                def _():
                    copy(here, here, self.down.at[b], self.recv.at[b], (blk, group)).wait_send()
                return carry
            lax.fori_loop(0, depth, body, 0)

    mine = role(me)
    kind = kind_of(me)

    barrier = pltpu.get_barrier_semaphore()
    peers(plane, me, lambda a: pl.semaphore_signal(
        barrier, inc=1, device_id=at_plane(a), device_id_type=pl.DeviceIdType.MESH))
    peers(depth, zed, lambda z: pl.semaphore_signal(
        barrier, inc=1, device_id=at_depth(z), device_id_type=pl.DeviceIdType.MESH))

    def embed(at):
        hidden = jnp.dot(staged[at], weights[at], preferred_element_type=F32)
        norm = jnp.sqrt(jnp.sum(hidden * hidden, axis=1, keepdims=True) + EPSILON)
        unit = hidden / norm
        units[at] = unit
        norms[at] = jnp.broadcast_to(norm, (rows, 128))
        return unit.astype(BF16)

    loads[1].wait()
    loads[3].wait()
    texts[zed] = embed(1)
    loads[0].wait()
    loads[2].wait()
    clips[me] = embed(0)
    feats[me] = staged[kind]
    pl.semaphore_wait(barrier, plane - 1 + depth - 1)

    text_chain = Chain(lambda z: texts.at[z], s_text, s_textd, r_text)
    text_chain.forward(zed)

    def send_clip(q):
        copy(clips.at[me], clips.at[me], s_clip.at[q], r_clip.at[me], at_plane(block_at(q, core))).start()
    peers(half, pos, send_clip)
    copy(clips.at[me], clips.at[me], s_clipf.at[pos], r_clip.at[me], sibling).start()

    def got(buf, at, recv, send):
        copy(buf.at[at], buf.at[at], send.at[0], recv.at[at], (blk, group)).wait_recv()

    def pass_clip(q):
        a = block_at(q, core)
        got(clips, a, r_clip, s_clip)
        copy(clips.at[a], clips.at[a], s_clipf.at[q], r_clip.at[a], sibling).start()
    nearest(text_chain.take, 1, min(2, depth))
    peers(half, pos, pass_clip)

    def send_feat(q):
        a = block_at(q, core)
        copy(staged.at[kind_of(a)], feats.at[me], s_feat.at[q], r_feat.at[me], at_plane(a)).start()
    peers(half, pos, send_feat)
    copy(staged.at[kind], feats.at[me], s_featf.at[pos], r_feat.at[me], sibling).start()

    nearest(text_chain.take, 2, min(3, depth))

    def take_clip(q, carry):
        got(clips, block_at(q, 1 - core), r_clip, s_clip)
        return carry
    lax.fori_loop(0, half, take_clip, 0)

    scale = scale_ref[0]
    bias = bias_ref[0]

    def all_clips():
        return clips[...].reshape(plane * rows, width)

    def columns(z):
        return pl.ds(pl.multiple_of(z * rows, rows), rows)

    def logits_of(z):
        return scale * lax.dot_general(all_clips(), texts[z], NT, preferred_element_type=F32) + bias

    def text_term(gate):
        return lax.dot_general(gate, all_clips(), TN, preferred_element_type=F32)

    logits = logits_of(zed)
    row = lax.broadcasted_iota(jnp.int32, logits.shape, 0)
    column = lax.broadcasted_iota(jnp.int32, logits.shape, 1)
    sign = jnp.where(row - column == me * rows, 1.0, -1.0)
    own_gate = (-sign / (1.0 + jnp.exp(sign * logits))).astype(BF16)
    gates[:, :, columns(zed)] = own_gate.reshape(plane, rows, rows)

    def text_step(z):
        gate = (1.0 / (1.0 + jnp.exp(-logits_of(z)))).astype(BF16)
        text_send[z] = text_term(gate).astype(BF16)
        copy(text_send.at[z], text_recv.at[zed], s_tg.at[z], r_tg.at[zed], at_depth(z)).start()
        gates[:, :, columns(z)] = gate.reshape(plane, rows, rows)

    def late_step(z):
        text_chain.take(z)
        text_step(z)
    nearest(text_step, 1, min(3, depth))
    nearest(late_step, 3, depth)

    def clip_term(a):
        return jnp.dot(gates[a], texts[...].reshape(depth * rows, width), preferred_element_type=F32)

    def give_clip(q, carry):
        clip_give[q] = clip_term(block_at(q, 1 - core)).astype(BF16)
        copy(clip_give.at[q], clip_take.at[q], s_give.at[q], r_give.at[q], sibling).start()
        return carry
    lax.fori_loop(0, half, give_clip, 0)

    def send_sum(q):
        term = clip_term(block_at(q, core))
        got(clip_take, q, r_give, s_give)
        clip_send[q] = (term + clip_take[q].astype(F32)).astype(BF16)
        copy(clip_send.at[q], clip_recv.at[pos], s_cg.at[q], r_cg.at[pos], at_plane(block_at(q, core))).start()
    peers(half, pos, send_sum)
    own_term = clip_term(me)
    got(clip_take, pos, r_give, s_give)
    clip_own[...] = own_term + clip_take[pos].astype(F32)

    def pass_feat(q):
        a = block_at(q, core)
        got(feats, a, r_feat, s_feat)
        copy(feats.at[a], feats.at[a], s_featf.at[q], r_feat.at[a], sibling).start()
    peers(half, pos, pass_feat)

    text_own[...] = text_term(gates[:, :, columns(zed)].reshape(plane * rows, rows))

    def backward(at, own, grad):
        unit = units[at]
        grad = scale * grad
        inner_sum = jnp.sum(unit * grad, axis=1, keepdims=True)
        result = (grad - unit * inner_sum) / norms[at][:, :1]
        for s in range(4):
            hid_send[4 * at + s] = result[:, s * lanes:(s + 1) * lanes]

    def add_clip(a):
        got(clip_recv, a, r_cg, s_cg)
        clip_own[...] += clip_recv[a].astype(F32)
    peers(half, pos, add_clip)
    backward(0, clip_own, clip_own[...])

    def send_hid(want, a):
        @pl.when(kind_of(a) == want)
        def _():
            copy(hid_send.at[role(a)], hid_recv.at[me], s_hid.at[a], r_hid.at[me], at_plane(a)).start()
    peers(plane, me, functools.partial(send_hid, 0))

    def add_text(z):
        got(text_recv, z, r_tg, s_tg)
        text_own[...] += text_recv[z].astype(F32)
    peers(depth, zed, add_text)
    backward(1, text_own, text_own[...])
    peers(plane, me, functools.partial(send_hid, 1))
    hid_recv[me] = hid_send[mine]

    def take_feat(q, carry):
        got(feats, block_at(q, 1 - core), r_feat, s_feat)
        return carry
    lax.fori_loop(0, half, take_feat, 0)
    peers(plane, me, lambda a: got(hid_recv, a, r_hid, s_hid))
    hidden = hid_recv[...].reshape(plane * rows, lanes)
    high = hidden.astype(BF16)
    low = (hidden - high.astype(F32)).astype(BF16)
    both = lax.dot_general(
        feats[...].reshape(plane * rows, feats.shape[2]),
        jnp.concatenate([high, low], axis=1), TN, preferred_element_type=F32)
    terms = (both[:, :lanes] + both[:, lanes:]).reshape(part_own.shape)
    part_own[...] = terms
    part_send[...] = terms.astype(BF16)

    def send_part(z):
        copy(part_send.at[z], part_recv.at[zed], s_part.at[z], r_part.at[zed], at_depth(z)).start()
    peers(depth, zed, send_part)
    part_recv[zed] = jnp.zeros(part_recv.shape[1:], BF16)

    def sent(src, send, recv, at):
        copy(src, src, send.at[at], recv.at[0], (blk, group)).wait_send()

    def drain_half(q, carry):
        sent(clips.at[me], s_clipf, r_clip, q)
        sent(staged.at[0], s_featf, r_feat, q)
        sent(clip_give.at[q], s_give, r_give, q)
        return carry
    lax.fori_loop(0, half, drain_half, 0)

    def drain_same(q):
        sent(clips.at[me], s_clip, r_clip, q)
        sent(staged.at[0], s_feat, r_feat, q)
        sent(clip_send.at[q], s_cg, r_cg, q)
    peers(half, pos, drain_same)
    peers(plane, me, lambda a: sent(hid_send.at[0], s_hid, r_hid, a))

    def drain_depth(z):
        sent(text_send.at[z], s_tg, r_tg, z)
    peers(depth, zed, drain_depth)

    text_chain.drain()
    peers(depth, zed, lambda z: got(part_recv, z, r_part, s_part))
    total = part_own[zed]
    for z in range(depth):
        total = total + part_recv[z].astype(F32)

    def rows_of(z):
        return pl.ds(pl.multiple_of(z * span, span), span)

    own = kind * 2 + lax.div(inner, 2)
    near = lax.div(group, 2) * 2
    gathered[core, own, rows_of(zed)] = total.astype(BF16)

    def same_core(q):
        return (zed * INNER + lax.rem(q, 2) * 2 + core, near + lax.div(q, 2))

    def spread(z):
        here = gathered.at[core, own, rows_of(z)]
        peers(4, own, lambda q: copy(here, here, s_agp.at[0], r_agp.at[z], same_core(q)).start())

    out_chain = Chain(lambda z: gathered.at[core, own, rows_of(z)], s_agz, s_agzd, r_agz)
    out_chain.forward(zed)
    spread(zed)

    def take_z(z):
        out_chain.take(z)
        spread(z)
    nearest(take_z, 1, depth)

    def relay(z):
        three = gathered.at[core, pl.ds(0, 3), rows_of(z)]
        copy(three, three, s_agp.at[0], r_agp.at[z], (blk, group)).wait_recv()
        here = gathered.at[core, :, rows_of(z)]
        copy(here, here, s_agc.at[z], r_agc.at[z], sibling).start()
    relay(zed)
    nearest(relay, 1, depth)

    def place(c):
        for q in range(4):
            at = pl.multiple_of(((q % 2) * 2 + c) * lanes, lanes)
            out[q // 2, :, pl.ds(at, lanes)] = gathered[c, q]
    place(core)

    def finish(k, carry):
        z = lax.rem(zed + k, depth)
        there = gathered.at[1 - core, :, rows_of(z)]
        copy(there, there, s_agc.at[z], r_agc.at[z], sibling).wait_recv()
        return carry
    lax.fori_loop(0, depth, finish, 0)
    place(1 - core)

    def drain_out(z):
        sent(part_send.at[z], s_part, r_part, z)
    peers(depth, zed, drain_out)
    out_chain.drain()
    sent(gathered.at[core, pl.ds(0, 3)], s_agp, r_agp, 0)

    def drain_relay(z, carry):
        sent(gathered.at[core, :, rows_of(z)], s_agc, r_agc, z)
        return carry
    lax.fori_loop(0, depth, drain_relay, 0)


def widen(grads_ref, audio_ref, text_ref):
    audio_ref[...] = grads_ref[0].astype(F32)
    text_ref[...] = grads_ref[1].astype(F32)


def per_device(blocks, groups, audio, audio_w, text, text_w, scale, bias):
    rows, wide = audio.shape
    width = audio_w.shape[1]
    depth, plane = blocks // INNER, INNER * groups
    lanes, span = width // 4, wide // depth
    vmem = pl.BlockSpec(memory_space=pltpu.VMEM)
    smem = pl.BlockSpec(memory_space=pltpu.SMEM)
    dma = pltpu.SemaphoreType.DMA
    half = plane // 2
    sems = [dma((count,)) for count in (
        4, half, half, plane, depth, depth, depth, half, half, plane, half, half, half, half, depth, depth,
        plane, plane, depth, depth, depth, depth, depth)]
    sems += [dma((count,)) for count in (1, depth, depth, depth)]
    whole = jax.ShapeDtypeStruct((2, wide, width), BF16)
    hbm = pl.BlockSpec(memory_space=pl.ANY)
    grads = pl.pallas_call(
        functools.partial(kernel, blocks, groups),
        out_shape=whole,
        in_specs=[hbm, hbm, hbm, hbm, smem, smem],
        out_specs=vmem,
        scratch_shapes=[
            pltpu.VMEM((plane, rows, width), BF16),
            pltpu.VMEM((depth, rows, width), BF16),
            pltpu.VMEM((2, rows, wide), BF16),
            pltpu.VMEM((2, wide, width), BF16),
            pltpu.VMEM((plane, rows, wide), BF16),
            pltpu.VMEM((plane, rows, depth * rows), BF16),
            pltpu.VMEM((half, rows, width), BF16),
            pltpu.VMEM((half, rows, width), BF16),
            pltpu.VMEM((half, rows, width), BF16),
            pltpu.VMEM((half, rows, width), BF16),
            pltpu.VMEM((depth, rows, width), BF16),
            pltpu.VMEM((depth, rows, width), BF16),
            pltpu.VMEM((rows, width), F32),
            pltpu.VMEM((rows, width), F32),
            pltpu.VMEM((2, rows, width), F32),
            pltpu.VMEM((2, rows, 128), F32),
            pltpu.VMEM((8, rows, lanes), F32),
            pltpu.VMEM((plane, rows, lanes), F32),
            pltpu.VMEM((depth, span, lanes), F32),
            pltpu.VMEM((depth, span, lanes), BF16),
            pltpu.VMEM((depth, span, lanes), BF16),
            pltpu.VMEM((2, 4, wide, lanes), BF16),
        ] + sems,
        compiler_params=pltpu.CompilerParams(
            collective_id=0, has_side_effects=True, vmem_limit_bytes=56 * 1024 * 1024),
    )(audio, audio_w, text, text_w, scale, bias)
    full = jax.ShapeDtypeStruct((wide, width), F32)
    step = wide // 4
    return pl.pallas_call(
        widen,
        out_shape=(full, full),
        grid=(4,),
        in_specs=[pl.BlockSpec((2, step, width), lambda i: (0, i, 0))],
        out_specs=(pl.BlockSpec((step, width), lambda i: (i, 0)),) * 2,
    )(grads)


def solution(mesh):
    placed = (P(("blk", "group"), None), P(), P(("blk", "group"), None), P(), P(), P())
    step = functools.partial(per_device, mesh.shape["blk"], mesh.shape["group"])
    return jax.shard_map(step, mesh=mesh, in_specs=placed, out_specs=(P(), P()), check_vma=False)
```

```python
import functools

import jax
import jax.numpy as jnp
from jax import lax
from jax.experimental import pallas as pl
from jax.experimental.pallas import tpu as pltpu
from jax.sharding import PartitionSpec as P

EPSILON = 1e-06
BF16 = jnp.bfloat16
F32 = jnp.float32
INNER = 4
TN = (((0,), (0,)), ((), ()))
NT = (((1,), (1,)), ((), ()))


def kernel(
    blocks, groups,
    audio_ref, audio_w_ref, text_ref, text_w_ref, scale_ref, bias_ref,
    out,
    clips, texts, staged, weights, feats, gates, clip_give, clip_take, clip_send, clip_recv, text_send, text_recv,
    clip_own, text_own, units, norms, hid_send, hid_recv, part_own, part_send, part_recv, gathered,
    s_in, s_clip, s_clipf, r_clip, s_text, r_text, s_feat, s_featf, r_feat, s_give, r_give, s_cg, r_cg, s_tg, r_tg,
    s_hid, r_hid, s_part, r_part, s_agz, r_agz, s_agp, r_agp, s_agc, r_agc,
):
    depth = blocks // INNER
    plane = INNER * groups
    rows = audio_ref.shape[0]
    width = audio_w_ref.shape[1]
    lanes = width // 4
    span = audio_w_ref.shape[0] // depth
    blk = lax.axis_index("blk")
    group = lax.axis_index("group")
    zed = lax.div(blk, INNER)
    inner = lax.rem(blk, INNER)
    me = inner * groups + group

    def at_plane(a):
        return (zed * INNER + lax.div(a, groups), lax.rem(a, groups))

    def at_depth(z):
        return (z * INNER + inner, group)

    half = plane // 2
    core = lax.rem(inner, 2)
    pos = lax.div(inner, 2) * groups + group
    sibling = (zed * INNER + inner + 1 - 2 * core, group)

    def block_at(q, c):
        return (lax.div(q, groups) * 2 + c) * groups + lax.rem(q, groups)

    def kind_of(a):
        return lax.rem(lax.rem(a, groups), 2)

    def role(a):
        return kind_of(a) * 4 + lax.div(a, groups)

    sources = (audio_ref, text_ref, audio_w_ref, text_w_ref)
    targets = (staged.at[0], staged.at[1], weights.at[0], weights.at[1])
    loads = [pltpu.make_async_copy(sources[k], targets[k], s_in.at[k]) for k in range(4)]
    for k in (1, 3, 0, 2):
        loads[k].start()

    def copy(src, dst, send, recv, device):
        return pltpu.make_async_remote_copy(
            src_ref=src, dst_ref=dst, send_sem=send, recv_sem=recv,
            device_id=device, device_id_type=pl.DeviceIdType.MESH,
        )

    def peers(count, own, fn):
        def body(k, carry):
            fn(lax.rem(own + k, count))
            return carry
        lax.fori_loop(1, count, body, 0)

    mine = role(me)
    kind = kind_of(me)

    barrier = pltpu.get_barrier_semaphore()
    peers(plane, me, lambda a: pl.semaphore_signal(
        barrier, inc=1, device_id=at_plane(a), device_id_type=pl.DeviceIdType.MESH))
    peers(depth, zed, lambda z: pl.semaphore_signal(
        barrier, inc=1, device_id=at_depth(z), device_id_type=pl.DeviceIdType.MESH))

    def embed(at):
        hidden = jnp.dot(staged[at], weights[at], preferred_element_type=F32)
        norm = jnp.sqrt(jnp.sum(hidden * hidden, axis=1, keepdims=True) + EPSILON)
        unit = hidden / norm
        units[at] = unit
        norms[at] = jnp.broadcast_to(norm, (rows, 128))
        return unit.astype(BF16)

    loads[1].wait()
    loads[3].wait()
    texts[zed] = embed(1)
    loads[0].wait()
    loads[2].wait()
    clips[me] = embed(0)
    feats[me] = staged[kind]
    pl.semaphore_wait(barrier, plane - 1 + depth - 1)

    def send_text(z):
        copy(texts.at[zed], texts.at[zed], s_text.at[z], r_text.at[zed], at_depth(z)).start()
    peers(depth, zed, send_text)

    def send_clip(q):
        copy(clips.at[me], clips.at[me], s_clip.at[q], r_clip.at[me], at_plane(block_at(q, core))).start()
    peers(half, pos, send_clip)
    copy(clips.at[me], clips.at[me], s_clipf.at[pos], r_clip.at[me], sibling).start()

    def got(buf, at, recv, send):
        copy(buf.at[at], buf.at[at], send.at[0], recv.at[at], (blk, group)).wait_recv()

    def pass_clip(q):
        a = block_at(q, core)
        got(clips, a, r_clip, s_clip)
        copy(clips.at[a], clips.at[a], s_clipf.at[q], r_clip.at[a], sibling).start()
    peers(half, pos, pass_clip)

    def send_feat(q):
        a = block_at(q, core)
        copy(staged.at[kind_of(a)], feats.at[me], s_feat.at[q], r_feat.at[me], at_plane(a)).start()
    peers(half, pos, send_feat)
    copy(staged.at[kind], feats.at[me], s_featf.at[pos], r_feat.at[me], sibling).start()

    def take_clip(q, carry):
        got(clips, block_at(q, 1 - core), r_clip, s_clip)
        return carry
    lax.fori_loop(0, half, take_clip, 0)

    scale = scale_ref[0]
    bias = bias_ref[0]

    def all_clips():
        return clips[...].reshape(plane * rows, width)

    def columns(z):
        return pl.ds(pl.multiple_of(z * rows, rows), rows)

    def logits_of(z):
        return scale * lax.dot_general(all_clips(), texts[z], NT, preferred_element_type=F32) + bias

    def text_term(gate):
        return lax.dot_general(gate, all_clips(), TN, preferred_element_type=F32)

    logits = logits_of(zed)
    row = lax.broadcasted_iota(jnp.int32, logits.shape, 0)
    column = lax.broadcasted_iota(jnp.int32, logits.shape, 1)
    sign = jnp.where(row - column == me * rows, 1.0, -1.0)
    own_gate = (-sign / (1.0 + jnp.exp(sign * logits))).astype(BF16)
    gates[:, :, columns(zed)] = own_gate.reshape(plane, rows, rows)

    def text_step(z):
        got(texts, z, r_text, s_text)
        gate = (1.0 / (1.0 + jnp.exp(-logits_of(z)))).astype(BF16)
        text_send[z] = text_term(gate).astype(BF16)
        copy(text_send.at[z], text_recv.at[zed], s_tg.at[z], r_tg.at[zed], at_depth(z)).start()
        gates[:, :, columns(z)] = gate.reshape(plane, rows, rows)
    peers(depth, zed, text_step)

    def clip_term(a):
        return jnp.dot(gates[a], texts[...].reshape(depth * rows, width), preferred_element_type=F32)

    def give_clip(q, carry):
        clip_give[q] = clip_term(block_at(q, 1 - core)).astype(BF16)
        copy(clip_give.at[q], clip_take.at[q], s_give.at[q], r_give.at[q], sibling).start()
        return carry
    lax.fori_loop(0, half, give_clip, 0)

    def send_sum(q):
        term = clip_term(block_at(q, core))
        got(clip_take, q, r_give, s_give)
        clip_send[q] = (term + clip_take[q].astype(F32)).astype(BF16)
        copy(clip_send.at[q], clip_recv.at[pos], s_cg.at[q], r_cg.at[pos], at_plane(block_at(q, core))).start()
    peers(half, pos, send_sum)
    own_term = clip_term(me)
    got(clip_take, pos, r_give, s_give)
    clip_own[...] = own_term + clip_take[pos].astype(F32)

    def pass_feat(q):
        a = block_at(q, core)
        got(feats, a, r_feat, s_feat)
        copy(feats.at[a], feats.at[a], s_featf.at[q], r_feat.at[a], sibling).start()
    peers(half, pos, pass_feat)

    text_own[...] = text_term(gates[:, :, columns(zed)].reshape(plane * rows, rows))

    def backward(at, own, grad):
        unit = units[at]
        grad = scale * grad
        inner_sum = jnp.sum(unit * grad, axis=1, keepdims=True)
        result = (grad - unit * inner_sum) / norms[at][:, :1]
        for s in range(4):
            hid_send[4 * at + s] = result[:, s * lanes:(s + 1) * lanes]

    def add_clip(a):
        got(clip_recv, a, r_cg, s_cg)
        clip_own[...] += clip_recv[a].astype(F32)
    peers(half, pos, add_clip)
    backward(0, clip_own, clip_own[...])

    def send_hid(want, a):
        @pl.when(kind_of(a) == want)
        def _():
            copy(hid_send.at[role(a)], hid_recv.at[me], s_hid.at[a], r_hid.at[me], at_plane(a)).start()
    peers(plane, me, functools.partial(send_hid, 0))

    def add_text(z):
        got(text_recv, z, r_tg, s_tg)
        text_own[...] += text_recv[z].astype(F32)
    peers(depth, zed, add_text)
    backward(1, text_own, text_own[...])
    peers(plane, me, functools.partial(send_hid, 1))
    hid_recv[me] = hid_send[mine]

    def take_feat(q, carry):
        got(feats, block_at(q, 1 - core), r_feat, s_feat)
        return carry
    lax.fori_loop(0, half, take_feat, 0)
    peers(plane, me, lambda a: got(hid_recv, a, r_hid, s_hid))
    hidden = hid_recv[...].reshape(plane * rows, lanes)
    high = hidden.astype(BF16)
    low = (hidden - high.astype(F32)).astype(BF16)
    both = lax.dot_general(
        feats[...].reshape(plane * rows, feats.shape[2]),
        jnp.concatenate([high, low], axis=1), TN, preferred_element_type=F32)
    terms = (both[:, :lanes] + both[:, lanes:]).reshape(part_own.shape)
    part_own[...] = terms
    part_send[...] = terms.astype(BF16)

    short = span // 2

    def half_rows(h):
        return pl.ds(h * short, short)

    def send_part(h, z):
        at = 2 * z + h
        copy(part_send.at[z, half_rows(h)], part_recv.at[zed, half_rows(h)],
             s_part.at[at], r_part.at[2 * zed + h], at_depth(z)).start()
    for h in range(2):
        peers(depth, zed, functools.partial(send_part, h))
    part_recv[zed] = jnp.zeros(part_recv.shape[1:], BF16)

    def sent(src, send, recv, at):
        copy(src, src, send.at[at], recv.at[0], (blk, group)).wait_send()

    def drain_half(q, carry):
        sent(clips.at[me], s_clipf, r_clip, q)
        sent(staged.at[0], s_featf, r_feat, q)
        sent(clip_give.at[q], s_give, r_give, q)
        return carry
    lax.fori_loop(0, half, drain_half, 0)

    def drain_same(q):
        sent(clips.at[me], s_clip, r_clip, q)
        sent(staged.at[0], s_feat, r_feat, q)
        sent(clip_send.at[q], s_cg, r_cg, q)
    peers(half, pos, drain_same)
    peers(plane, me, lambda a: sent(hid_send.at[0], s_hid, r_hid, a))

    def drain_depth(z):
        sent(texts.at[zed], s_text, r_text, z)
        sent(text_send.at[z], s_tg, r_tg, z)
    peers(depth, zed, drain_depth)

    def rows_of(z, h):
        return pl.ds(pl.multiple_of(z * span + h * short, short), short)

    own = kind * 2 + lax.div(inner, 2)
    near = lax.div(group, 2) * 2

    def same_core(q):
        return (zed * INNER + lax.rem(q, 2) * 2 + core, near + lax.div(q, 2))

    def spread(h, z):
        here = gathered.at[core, own, rows_of(z, h)]
        at = 2 * z + h
        peers(4, own, lambda q: copy(here, here, s_agp.at[0], r_agp.at[at], same_core(q)).start())

    def take_part(h, z):
        here = part_recv.at[z, half_rows(h)]
        copy(here, here, s_part.at[0], r_part.at[2 * z + h], (blk, group)).wait_recv()

    def send_z(h, z):
        here = gathered.at[core, own, rows_of(zed, h)]
        copy(here, here, s_agz.at[2 * z + h], r_agz.at[2 * zed + h], at_depth(z)).start()

    def take_z(h, z):
        here = gathered.at[core, own, rows_of(z, h)]
        copy(here, here, s_agz.at[2 * z + h], r_agz.at[2 * z + h], (blk, group)).wait_recv()
        spread(h, z)

    def relay(h, k, carry):
        z = lax.rem(zed + k, depth)
        at = 2 * z + h
        three = gathered.at[core, pl.ds(0, 3), rows_of(z, h)]
        copy(three, three, s_agp.at[0], r_agp.at[at], (blk, group)).wait_recv()
        here = gathered.at[core, :, rows_of(z, h)]
        copy(here, here, s_agc.at[at], r_agc.at[at], sibling).start()
        return carry

    for h in range(2):
        peers(depth, zed, functools.partial(take_part, h))
        total = part_own[zed, h * short:(h + 1) * short]
        for z in range(depth):
            total = total + part_recv[z, h * short:(h + 1) * short].astype(F32)
        gathered[core, own, rows_of(zed, h)] = total.astype(BF16)
        peers(depth, zed, functools.partial(send_z, h))
        spread(h, zed)
    for h in range(2):
        peers(depth, zed, functools.partial(take_z, h))
    for h in range(2):
        lax.fori_loop(0, depth, functools.partial(relay, h), 0)

    def place(c):
        for q in range(4):
            at = pl.multiple_of(((q % 2) * 2 + c) * lanes, lanes)
            out[q // 2, :, pl.ds(at, lanes)] = gathered[c, q]
    place(core)

    def finish(h, k, carry):
        z = lax.rem(zed + k, depth)
        there = gathered.at[1 - core, :, rows_of(z, h)]
        copy(there, there, s_agc.at[2 * z + h], r_agc.at[2 * z + h], sibling).wait_recv()
        return carry
    for h in range(2):
        lax.fori_loop(0, depth, functools.partial(finish, h), 0)
    place(1 - core)

    def drain_out(h, z):
        sent(part_send.at[z, half_rows(h)], s_part, r_part, 2 * z + h)
        sent(gathered.at[core, own, rows_of(zed, h)], s_agz, r_agz, 2 * z + h)

    def drain_relay(h, z, carry):
        sent(gathered.at[core, :, rows_of(z, h)], s_agc, r_agc, 2 * z + h)
        return carry
    for h in range(2):
        peers(depth, zed, functools.partial(drain_out, h))
        lax.fori_loop(0, depth, functools.partial(drain_relay, h), 0)
    sent(gathered.at[core, pl.ds(0, 3)], s_agp, r_agp, 0)


def per_device(blocks, groups, audio, audio_w, text, text_w, scale, bias):
    rows, wide = audio.shape
    width = audio_w.shape[1]
    depth, plane = blocks // INNER, INNER * groups
    lanes, span = width // 4, wide // depth
    vmem = pl.BlockSpec(memory_space=pltpu.VMEM)
    smem = pl.BlockSpec(memory_space=pltpu.SMEM)
    dma = pltpu.SemaphoreType.DMA
    half = plane // 2
    sems = [dma((count,)) for count in (
        4, half, half, plane, depth, depth, half, half, plane, half, half, half, half, depth, depth,
        plane, plane, 2 * depth, 2 * depth, 2 * depth, 2 * depth)]
    sems += [dma((count,)) for count in (1, 2 * depth, 2 * depth, 2 * depth)]
    whole = jax.ShapeDtypeStruct((2, wide, width), BF16)
    hbm = pl.BlockSpec(memory_space=pl.ANY)
    grads = pl.pallas_call(
        functools.partial(kernel, blocks, groups),
        out_shape=whole,
        in_specs=[hbm, hbm, hbm, hbm, smem, smem],
        out_specs=vmem,
        scratch_shapes=[
            pltpu.VMEM((plane, rows, width), BF16),
            pltpu.VMEM((depth, rows, width), BF16),
            pltpu.VMEM((2, rows, wide), BF16),
            pltpu.VMEM((2, wide, width), BF16),
            pltpu.VMEM((plane, rows, wide), BF16),
            pltpu.VMEM((plane, rows, depth * rows), BF16),
            pltpu.VMEM((half, rows, width), BF16),
            pltpu.VMEM((half, rows, width), BF16),
            pltpu.VMEM((half, rows, width), BF16),
            pltpu.VMEM((half, rows, width), BF16),
            pltpu.VMEM((depth, rows, width), BF16),
            pltpu.VMEM((depth, rows, width), BF16),
            pltpu.VMEM((rows, width), F32),
            pltpu.VMEM((rows, width), F32),
            pltpu.VMEM((2, rows, width), F32),
            pltpu.VMEM((2, rows, 128), F32),
            pltpu.VMEM((8, rows, lanes), F32),
            pltpu.VMEM((plane, rows, lanes), F32),
            pltpu.VMEM((depth, span, lanes), F32),
            pltpu.VMEM((depth, span, lanes), BF16),
            pltpu.VMEM((depth, span, lanes), BF16),
            pltpu.VMEM((2, 4, wide, lanes), BF16),
        ] + sems,
        compiler_params=pltpu.CompilerParams(
            collective_id=0, has_side_effects=True, vmem_limit_bytes=56 * 1024 * 1024),
    )(audio, audio_w, text, text_w, scale, bias)
    return grads[0].astype(F32), grads[1].astype(F32)


def solution(mesh):
    placed = (P(("blk", "group"), None), P(), P(("blk", "group"), None), P(), P(), P())
    step = functools.partial(per_device, mesh.shape["blk"], mesh.shape["group"])
    return jax.shard_map(step, mesh=mesh, in_specs=placed, out_specs=(P(), P()), check_vma=False)
```

```python
import functools

import jax
import jax.numpy as jnp
from jax import lax
from jax.experimental import pallas as pl
from jax.experimental.pallas import tpu as pltpu
from jax.sharding import PartitionSpec as P

EPSILON = 1e-06
BF16 = jnp.bfloat16
F32 = jnp.float32
INNER = 4
TN = (((0,), (0,)), ((), ()))
NT = (((1,), (1,)), ((), ()))


def kernel(
    blocks, groups,
    audio_ref, audio_w_ref, text_ref, text_w_ref, scale_ref, bias_ref,
    out,
    clips, texts, staged, weights, feats, gates, clip_give, clip_take, clip_send, clip_recv, text_send, text_recv,
    clip_own, text_own, units, norms, hid_send, hid_recv, part_own, part_send, part_recv, gathered,
    s_in, s_clip, s_clipf, r_clip, s_text, r_text, s_feat, s_featf, r_feat, s_give, r_give, s_cg, r_cg, s_tg, r_tg,
    s_hid, r_hid, s_part, r_part, s_agz, r_agz, s_agp, r_agp, s_agc, r_agc,
):
    depth = blocks // INNER
    plane = INNER * groups
    rows = audio_ref.shape[0]
    width = audio_w_ref.shape[1]
    lanes = width // 4
    span = audio_w_ref.shape[0] // depth
    blk = lax.axis_index("blk")
    group = lax.axis_index("group")
    zed = lax.div(blk, INNER)
    inner = lax.rem(blk, INNER)
    me = inner * groups + group

    def at_plane(a):
        return (zed * INNER + lax.div(a, groups), lax.rem(a, groups))

    def at_depth(z):
        return (z * INNER + inner, group)

    half = plane // 2
    core = lax.rem(inner, 2)
    pos = lax.div(inner, 2) * groups + group
    sibling = (zed * INNER + inner + 1 - 2 * core, group)

    def block_at(q, c):
        return (lax.div(q, groups) * 2 + c) * groups + lax.rem(q, groups)

    def kind_of(a):
        return lax.rem(lax.rem(a, groups), 2)

    def role(a):
        return kind_of(a) * 4 + lax.div(a, groups)

    sources = (audio_ref, text_ref, audio_w_ref, text_w_ref)
    targets = (staged.at[0], staged.at[1], weights.at[0], weights.at[1])
    loads = [pltpu.make_async_copy(sources[k], targets[k], s_in.at[k]) for k in range(4)]
    for k in (1, 3, 0, 2):
        loads[k].start()

    def copy(src, dst, send, recv, device):
        return pltpu.make_async_remote_copy(
            src_ref=src, dst_ref=dst, send_sem=send, recv_sem=recv,
            device_id=device, device_id_type=pl.DeviceIdType.MESH,
        )

    def peers(count, own, fn):
        def body(k, carry):
            fn(lax.rem(own + k, count))
            return carry
        lax.fori_loop(1, count, body, 0)

    mine = role(me)
    kind = kind_of(me)

    barrier = pltpu.get_barrier_semaphore()
    peers(plane, me, lambda a: pl.semaphore_signal(
        barrier, inc=1, device_id=at_plane(a), device_id_type=pl.DeviceIdType.MESH))
    peers(depth, zed, lambda z: pl.semaphore_signal(
        barrier, inc=1, device_id=at_depth(z), device_id_type=pl.DeviceIdType.MESH))

    def embed(at):
        hidden = jnp.dot(staged[at], weights[at], preferred_element_type=F32)
        norm = jnp.sqrt(jnp.sum(hidden * hidden, axis=1, keepdims=True) + EPSILON)
        unit = hidden / norm
        units[at] = unit
        norms[at] = jnp.broadcast_to(norm, (rows, 128))
        return unit.astype(BF16)

    loads[1].wait()
    loads[3].wait()
    texts[zed] = embed(1)
    loads[0].wait()
    loads[2].wait()
    clips[me] = embed(0)
    feats[me] = staged[kind]
    pl.semaphore_wait(barrier, plane - 1 + depth - 1)

    def send_text(z):
        copy(texts.at[zed], texts.at[zed], s_text.at[z], r_text.at[zed], at_depth(z)).start()
    peers(depth, zed, send_text)

    def send_clip(q):
        copy(clips.at[me], clips.at[me], s_clip.at[q], r_clip.at[me], at_plane(block_at(q, core))).start()
    peers(half, pos, send_clip)
    copy(clips.at[me], clips.at[me], s_clipf.at[pos], r_clip.at[me], sibling).start()

    def got(buf, at, recv, send):
        copy(buf.at[at], buf.at[at], send.at[0], recv.at[at], (blk, group)).wait_recv()

    def pass_clip(q):
        a = block_at(q, core)
        got(clips, a, r_clip, s_clip)
        copy(clips.at[a], clips.at[a], s_clipf.at[q], r_clip.at[a], sibling).start()
    peers(half, pos, pass_clip)

    def send_feat(q):
        a = block_at(q, core)
        copy(staged.at[kind_of(a)], feats.at[me], s_feat.at[q], r_feat.at[me], at_plane(a)).start()
    peers(half, pos, send_feat)
    copy(staged.at[kind], feats.at[me], s_featf.at[pos], r_feat.at[me], sibling).start()

    def take_clip(q, carry):
        got(clips, block_at(q, 1 - core), r_clip, s_clip)
        return carry
    lax.fori_loop(0, half, take_clip, 0)

    scale = scale_ref[0]
    bias = bias_ref[0]

    def all_clips():
        return clips[...].reshape(plane * rows, width)

    def columns(z):
        return pl.ds(pl.multiple_of(z * rows, rows), rows)

    def logits_of(z):
        return scale * lax.dot_general(all_clips(), texts[z], NT, preferred_element_type=F32) + bias

    def text_term(gate):
        return lax.dot_general(gate, all_clips(), TN, preferred_element_type=F32)

    logits = logits_of(zed)
    row = lax.broadcasted_iota(jnp.int32, logits.shape, 0)
    column = lax.broadcasted_iota(jnp.int32, logits.shape, 1)
    sign = jnp.where(row - column == me * rows, 1.0, -1.0)
    own_gate = (-sign / (1.0 + jnp.exp(sign * logits))).astype(BF16)
    gates[:, :, columns(zed)] = own_gate.reshape(plane, rows, rows)

    def text_step(z):
        got(texts, z, r_text, s_text)
        gate = (1.0 / (1.0 + jnp.exp(-logits_of(z)))).astype(BF16)
        text_send[z] = text_term(gate).astype(BF16)
        copy(text_send.at[z], text_recv.at[zed], s_tg.at[z], r_tg.at[zed], at_depth(z)).start()
        gates[:, :, columns(z)] = gate.reshape(plane, rows, rows)
    peers(depth, zed, text_step)

    def clip_term(a):
        return jnp.dot(gates[a], texts[...].reshape(depth * rows, width), preferred_element_type=F32)

    def give_clip(q):
        clip_give[q] = clip_term(block_at(q, 1 - core)).astype(BF16)
        copy(clip_give.at[q], clip_take.at[q], s_give.at[q], r_give.at[q], sibling).start()
    peers(half, pos, give_clip)
    give_clip(pos)

    def send_sum(q):
        term = clip_term(block_at(q, core))
        got(clip_take, q, r_give, s_give)
        clip_send[q] = (term + clip_take[q].astype(F32)).astype(BF16)
        copy(clip_send.at[q], clip_recv.at[pos], s_cg.at[q], r_cg.at[pos], at_plane(block_at(q, core))).start()
    peers(half, pos, send_sum)
    own_term = clip_term(me)
    got(clip_take, pos, r_give, s_give)
    clip_own[...] = own_term + clip_take[pos].astype(F32)

    text_own[...] = text_term(gates[:, :, columns(zed)].reshape(plane * rows, rows))

    def backward(at, own, grad):
        unit = units[at]
        grad = scale * grad
        inner_sum = jnp.sum(unit * grad, axis=1, keepdims=True)
        result = (grad - unit * inner_sum) / norms[at][:, :1]
        for s in range(4):
            hid_send[4 * at + s] = result[:, s * lanes:(s + 1) * lanes]

    def add_clip(a):
        got(clip_recv, a, r_cg, s_cg)
        clip_own[...] += clip_recv[a].astype(F32)
    peers(half, pos, add_clip)
    backward(0, clip_own, clip_own[...])

    def send_hid(want, a):
        @pl.when(kind_of(a) == want)
        def _():
            copy(hid_send.at[role(a)], hid_recv.at[me], s_hid.at[a], r_hid.at[me], at_plane(a)).start()
    peers(plane, me, functools.partial(send_hid, 0))

    def pass_feat(q):
        a = block_at(q, core)
        got(feats, a, r_feat, s_feat)
        copy(feats.at[a], feats.at[a], s_featf.at[q], r_feat.at[a], sibling).start()
    peers(half, pos, pass_feat)

    def add_text(z):
        got(text_recv, z, r_tg, s_tg)
        text_own[...] += text_recv[z].astype(F32)
    peers(depth, zed, add_text)
    backward(1, text_own, text_own[...])
    peers(plane, me, functools.partial(send_hid, 1))
    hid_recv[me] = hid_send[mine]

    def take_feat(q, carry):
        got(feats, block_at(q, 1 - core), r_feat, s_feat)
        return carry
    lax.fori_loop(0, half, take_feat, 0)
    peers(plane, me, lambda a: got(hid_recv, a, r_hid, s_hid))
    hidden = hid_recv[...].reshape(plane * rows, lanes)
    high = hidden.astype(BF16)
    low = (hidden - high.astype(F32)).astype(BF16)
    both = lax.dot_general(
        feats[...].reshape(plane * rows, feats.shape[2]),
        jnp.concatenate([high, low], axis=1), TN, preferred_element_type=F32)
    terms = (both[:, :lanes] + both[:, lanes:]).reshape(part_own.shape)
    part_own[...] = terms
    part_send[...] = terms.astype(BF16)

    short = span // 2

    def half_rows(h):
        return pl.ds(h * short, short)

    def send_part(h, z):
        at = 2 * z + h
        copy(part_send.at[z, half_rows(h)], part_recv.at[zed, half_rows(h)],
             s_part.at[at], r_part.at[2 * zed + h], at_depth(z)).start()
    for h in range(2):
        peers(depth, zed, functools.partial(send_part, h))
    part_recv[zed] = jnp.zeros(part_recv.shape[1:], BF16)

    def sent(src, send, recv, at):
        copy(src, src, send.at[at], recv.at[0], (blk, group)).wait_send()

    def drain_half(q, carry):
        sent(clips.at[me], s_clipf, r_clip, q)
        sent(staged.at[0], s_featf, r_feat, q)
        sent(clip_give.at[q], s_give, r_give, q)
        return carry
    lax.fori_loop(0, half, drain_half, 0)

    def drain_same(q):
        sent(clips.at[me], s_clip, r_clip, q)
        sent(staged.at[0], s_feat, r_feat, q)
        sent(clip_send.at[q], s_cg, r_cg, q)
    peers(half, pos, drain_same)
    peers(plane, me, lambda a: sent(hid_send.at[0], s_hid, r_hid, a))

    def drain_depth(z):
        sent(texts.at[zed], s_text, r_text, z)
        sent(text_send.at[z], s_tg, r_tg, z)
    peers(depth, zed, drain_depth)

    def rows_of(z, h):
        return pl.ds(pl.multiple_of(z * span + h * short, short), short)

    own = kind * 2 + lax.div(inner, 2)
    near = lax.div(group, 2) * 2

    def same_core(q):
        return (zed * INNER + lax.rem(q, 2) * 2 + core, near + lax.div(q, 2))

    def spread(h, z):
        here = gathered.at[core, own, rows_of(z, h)]
        at = 2 * z + h
        peers(4, own, lambda q: copy(here, here, s_agp.at[0], r_agp.at[at], same_core(q)).start())

    def take_part(h, z):
        here = part_recv.at[z, half_rows(h)]
        copy(here, here, s_part.at[0], r_part.at[2 * z + h], (blk, group)).wait_recv()

    def send_z(h, z):
        here = gathered.at[core, own, rows_of(zed, h)]
        copy(here, here, s_agz.at[2 * z + h], r_agz.at[2 * zed + h], at_depth(z)).start()

    def take_z(h, z):
        here = gathered.at[core, own, rows_of(z, h)]
        copy(here, here, s_agz.at[2 * z + h], r_agz.at[2 * z + h], (blk, group)).wait_recv()
        spread(h, z)

    def relay(h, k, carry):
        z = lax.rem(zed + k, depth)
        at = 2 * z + h
        three = gathered.at[core, pl.ds(0, 3), rows_of(z, h)]
        copy(three, three, s_agp.at[0], r_agp.at[at], (blk, group)).wait_recv()
        here = gathered.at[core, :, rows_of(z, h)]
        copy(here, here, s_agc.at[at], r_agc.at[at], sibling).start()
        return carry

    for h in range(2):
        peers(depth, zed, functools.partial(take_part, h))
        total = part_own[zed, h * short:(h + 1) * short]
        for z in range(depth):
            total = total + part_recv[z, h * short:(h + 1) * short].astype(F32)
        gathered[core, own, rows_of(zed, h)] = total.astype(BF16)
        peers(depth, zed, functools.partial(send_z, h))
        spread(h, zed)
    for h in range(2):
        peers(depth, zed, functools.partial(take_z, h))
    for h in range(2):
        lax.fori_loop(0, depth, functools.partial(relay, h), 0)

    def place(c):
        for q in range(4):
            at = pl.multiple_of(((q % 2) * 2 + c) * lanes, lanes)
            out[q // 2, :, pl.ds(at, lanes)] = gathered[c, q]
    place(core)

    def finish(h, k, carry):
        z = lax.rem(zed + k, depth)
        there = gathered.at[1 - core, :, rows_of(z, h)]
        copy(there, there, s_agc.at[2 * z + h], r_agc.at[2 * z + h], sibling).wait_recv()
        return carry
    for h in range(2):
        lax.fori_loop(0, depth, functools.partial(finish, h), 0)
    place(1 - core)

    def drain_out(h, z):
        sent(part_send.at[z, half_rows(h)], s_part, r_part, 2 * z + h)
        sent(gathered.at[core, own, rows_of(zed, h)], s_agz, r_agz, 2 * z + h)

    def drain_relay(h, z, carry):
        sent(gathered.at[core, :, rows_of(z, h)], s_agc, r_agc, 2 * z + h)
        return carry
    for h in range(2):
        peers(depth, zed, functools.partial(drain_out, h))
        lax.fori_loop(0, depth, functools.partial(drain_relay, h), 0)
    sent(gathered.at[core, pl.ds(0, 3)], s_agp, r_agp, 0)


def per_device(blocks, groups, audio, audio_w, text, text_w, scale, bias):
    rows, wide = audio.shape
    width = audio_w.shape[1]
    depth, plane = blocks // INNER, INNER * groups
    lanes, span = width // 4, wide // depth
    vmem = pl.BlockSpec(memory_space=pltpu.VMEM)
    smem = pl.BlockSpec(memory_space=pltpu.SMEM)
    dma = pltpu.SemaphoreType.DMA
    half = plane // 2
    sems = [dma((count,)) for count in (
        4, half, half, plane, depth, depth, half, half, plane, half, half, half, half, depth, depth,
        plane, plane, 2 * depth, 2 * depth, 2 * depth, 2 * depth)]
    sems += [dma((count,)) for count in (1, 2 * depth, 2 * depth, 2 * depth)]
    whole = jax.ShapeDtypeStruct((2, wide, width), BF16)
    hbm = pl.BlockSpec(memory_space=pl.ANY)
    grads = pl.pallas_call(
        functools.partial(kernel, blocks, groups),
        out_shape=whole,
        in_specs=[hbm, hbm, hbm, hbm, smem, smem],
        out_specs=vmem,
        scratch_shapes=[
            pltpu.VMEM((plane, rows, width), BF16),
            pltpu.VMEM((depth, rows, width), BF16),
            pltpu.VMEM((2, rows, wide), BF16),
            pltpu.VMEM((2, wide, width), BF16),
            pltpu.VMEM((plane, rows, wide), BF16),
            pltpu.VMEM((plane, rows, depth * rows), BF16),
            pltpu.VMEM((half, rows, width), BF16),
            pltpu.VMEM((half, rows, width), BF16),
            pltpu.VMEM((half, rows, width), BF16),
            pltpu.VMEM((half, rows, width), BF16),
            pltpu.VMEM((depth, rows, width), BF16),
            pltpu.VMEM((depth, rows, width), BF16),
            pltpu.VMEM((rows, width), F32),
            pltpu.VMEM((rows, width), F32),
            pltpu.VMEM((2, rows, width), F32),
            pltpu.VMEM((2, rows, 128), F32),
            pltpu.VMEM((8, rows, lanes), F32),
            pltpu.VMEM((plane, rows, lanes), F32),
            pltpu.VMEM((depth, span, lanes), F32),
            pltpu.VMEM((depth, span, lanes), BF16),
            pltpu.VMEM((depth, span, lanes), BF16),
            pltpu.VMEM((2, 4, wide, lanes), BF16),
        ] + sems,
        compiler_params=pltpu.CompilerParams(
            collective_id=0, has_side_effects=True, vmem_limit_bytes=56 * 1024 * 1024),
    )(audio, audio_w, text, text_w, scale, bias)
    return grads[0].astype(F32), grads[1].astype(F32)


def solution(mesh):
    placed = (P(("blk", "group"), None), P(), P(("blk", "group"), None), P(), P(), P())
    step = functools.partial(per_device, mesh.shape["blk"], mesh.shape["group"])
    return jax.shard_map(step, mesh=mesh, in_specs=placed, out_specs=(P(), P()), check_vma=False)
```
